256 devices in a mesh: seq: 16 (over y, x), grp: 8 (over z), store: 2 (over core).
Axes of the slice: x: 4, y: 4, z: 8, core: 2. Of those that a mesh axis runs over, the one named last changes fastest.
Arguments:
- query: bfloat16 [8, 2, 32, 2048, 128], P('grp', 'store', None, 'seq')
- kv_store: bfloat16 [256, 2, 2, 32, 128, 128], P(('grp', 'store'), None, None, 'seq'), may hold values from -6 to 6
- nbr_owner: int32 [8, 32, 2], P('grp'), may hold values from 0 to 15, all different within a row; in each aligned block of 32 rows (0 to 31, 32 to 63, ..., all dimensions but the last counted through in order) at most 6 rows name the same one
- nbr_block: int32 [8, 32, 2], P('grp'), may hold values from 0 to 15
- d_out: bfloat16 [8, 2, 32, 2048, 128], P('grp', 'store', None, 'seq'), may hold values from -6 to 6
Outputs:
- attn_out: bfloat16 [8, 2, 32, 2048, 128], P('grp', 'store', None, 'seq')
- d_query: bfloat16 [8, 2, 32, 2048, 128], P('grp', 'store', None, 'seq')
- d_kv: bfloat16 [256, 2, 2, 32, 128, 128], P(('grp', 'store'), None, None, 'seq')
The draws below stay inside these ranges and needn't reach their ends.
Inputs may be any that keep to these rules, and one draw needn't show every extreme that they name: `nbr_owner`: among one group's 32 spans no store shard is named more than 6 times, a bound that some block reaches; the 2 neighbours of a span lie in different shards; every shard is named somewhere.
All inputs are finite; a program needn't handle non-finite values.
Results may differ from the reference program's by a relative error of at most 0.027.
Values may be sent and summed in bfloat16 or wider, within the bound.
No kernel may reach another device: no remote copies, remote signals or barrier semaphores. Data moves between devices by JAX's collectives and lax.ppermute only.
A program may use at most 128 MiB of HBM per device.

```python
import math
import jax
import jax.numpy as jnp
import numpy as np
from jax import lax

D = 8192
H = 64
DH = 128
SPAN = 64
NBR_LEN = 128
NBRS = 2
BLK_DEV = 16
GROUPS = 8
GROUP_TOK = 2048
GROUP_SPANS = 32
OWNERS = 16
BLOCKS = 256
CAPACITY = 6


def draw_query(key, part):
    key = jax.random.fold_in(key, 7)
    shape = (GROUPS, 2, H // 2, GROUP_TOK, D // H)
    return jax.random.normal(key, shape, jnp.float32).astype(jnp.bfloat16)


def set_ends(result, rng, low, high):
    longest = result.shape.index(max(result.shape))
    spots = []
    for shift in (0, 1):
        where = [jax.random.randint(jax.random.fold_in(rng, axis), (), 0, length) for axis, length in enumerate(result.shape)]
        where[longest] = (where[longest] + shift) % result.shape[longest]
        spots.append(tuple(where))
    return result.at[spots[0]].set(low).at[spots[1]].set(high)


def block_scale(stream_key, extent, pieces, least, high):
    def one(axis_at, shards_of):
        draws = jax.random.uniform(jax.random.fold_in(jax.random.fold_in(stream_key, 6), axis_at), (shards_of,), jnp.float32, least / len(pieces), high / len(pieces))
        return jnp.repeat(jnp.exp(draws), extent[axis_at] // shards_of).reshape((-1,) + (1,) * (len(extent) - axis_at - 1))

    level = one(*pieces[0])
    for cut in pieces[1:]:
        level = level * one(*cut)
    return level


def shared_out(own_key, own, number, rows, amount, top, most, skew):
    order = jax.random.permutation(own_key, amount)
    crowded, usual = load_shares(amount, rows * top, most, skew, True), load_shares(amount, rows * top, most, skew, False)
    places = jnp.arange(amount)

    def named(lengths, offset_by):
        used = int((lengths > 0).sum())
        fixed = max(1, used // 4)
        moved = fixed + (places - fixed + offset_by * (used - fixed)) % max(1, amount - fixed)
        return jnp.zeros((amount,), jnp.int32).at[order[jnp.where(places < fixed, places, moved)]].set(jnp.asarray(lengths, jnp.int32))

    lengths = jnp.where(number % 4 == 0, named(crowded, number // 4), named(usual, number - number // 4 - 1))
    mixed = jax.random.permutation(jax.random.fold_in(own, 3), amount)
    source_of, taker = mixed[0:amount // 2 * 2:2], mixed[1:amount // 2 * 2:2]
    slack = jnp.minimum(lengths[source_of] - 1, most - lengths[taker]) // 2
    slack = jnp.where((source_of == order[0]) | (taker == order[0]) | (lengths[taker] == 0), 0, jnp.maximum(slack, 0))
    moved = jax.random.randint(jax.random.fold_in(own, 4), (amount // 2,), 0, 1 << 20) % (slack + 1)
    lengths = lengths.at[source_of].add(-moved).at[taker].add(moved)
    labels = jnp.searchsorted(jnp.cumsum(lengths), jnp.arange(rows * top), side="right").astype(jnp.int32)
    table = labels.reshape(top, rows).T
    table = table[jax.random.permutation(jax.random.fold_in(own, 1), rows)]
    offset_by = jax.random.randint(jax.random.fold_in(own, 2), (rows, 1), 0, top)
    return jnp.take_along_axis(table, (jnp.arange(top)[None, :] + offset_by) % top, axis=1)


def load_shares(number_of, total, most, slope, full):
    portions = [(1 << 20) // math.isqrt(grade ** slope) + 1 for grade in range(1, number_of + 1)]
    largest = most if full else min(most, max(-(-total // number_of), total * portions[0] // sum(portions)))
    least = 1 if total - largest >= number_of - 1 else 0
    given, surplus = [largest] + [least] * (number_of - 1), total - largest - least * (number_of - 1)
    while surplus > 0:
        free = [i for i in range(1, number_of) if given[i] < largest] or [i for i in range(1, number_of) if given[i] < most]
        pool, left = sum([portions[i] for i in free]), surplus
        for i in free:
            addition = min(most - given[i], max(1, left * portions[i] // pool), surplus)
            given[i] = given[i] + addition
            surplus = surplus - addition
    return np.array(given)


def bell_draw(key, extent, width, reach, shards=(), dtype=jnp.bfloat16):
    entries = width * jax.random.normal(key, extent, jnp.float32)
    if shards:
        entries = entries * block_scale(key, extent, shards, -0.22, 0.18)
    return jnp.clip(entries, -reach, reach).astype(dtype)


def setup_inputs(seed: int = 0) -> dict:
    arg_keys = jax.random.split(jax.random.key(seed), 6)
    query = draw_query(jax.random.fold_in(arg_keys[5], 71), 0)
    kv_store = bell_draw(arg_keys[1], (BLOCKS, 2, 2, H // 2, NBR_LEN, DH), 1.0, 6.0, ((0, 16), (3, 16)))
    nbr_owner_keys = jax.random.split(jax.random.fold_in(arg_keys[2], 1), GROUPS * GROUP_SPANS // GROUP_SPANS)
    nbr_owner_turns = jax.random.permutation(jax.random.fold_in(arg_keys[2], 3), GROUPS * GROUP_SPANS // GROUP_SPANS)
    nbr_owner = jax.vmap(lambda own, number: shared_out(jax.random.fold_in(arg_keys[2], 2), own, number, GROUP_SPANS, OWNERS, NBRS, CAPACITY, 2))(nbr_owner_keys, nbr_owner_turns).reshape((GROUPS, GROUP_SPANS, NBRS))
    nbr_block = set_ends(jax.random.randint(arg_keys[3], (GROUPS, GROUP_SPANS, NBRS), 0, BLK_DEV), jax.random.fold_in(arg_keys[3], 1), 0, BLK_DEV - 1).astype(jnp.int32)
    d_out = bell_draw(arg_keys[4], (GROUPS, 2, H // 2, GROUP_TOK, DH), 1.0, 6.0, ((0, 8), (1, 2), (3, 16)))
    return {"query": query, "kv_store": kv_store, "nbr_owner": nbr_owner, "nbr_block": nbr_block, "d_out": d_out}


def reference(query, kv_store, nbr_owner, nbr_block, d_out):
    score_scale = 1.0 / math.sqrt(DH)
    grad_start = jnp.zeros(kv_store.shape, jnp.float32)

    def per_group(grad_store, group_items):
        group_query, group_owner, group_block, group_grad = group_items
        query_rows = jnp.transpose(group_query, (2, 1, 0, 3)).reshape(GROUP_SPANS, SPAN, H, DH).astype(jnp.float32)
        grad_rows = jnp.transpose(group_grad, (2, 1, 0, 3)).reshape(GROUP_SPANS, SPAN, H, DH).astype(jnp.float32)
        block_ids = (group_owner.astype(jnp.int32) * BLK_DEV + group_block.astype(jnp.int32)).reshape(-1)
        picked = jnp.transpose(kv_store[block_ids], (0, 4, 3, 2, 1, 5))
        context = picked.reshape(GROUP_SPANS, NBRS * NBR_LEN, H, 2, DH)
        key_rows = context[:, :, :, 0, :].astype(jnp.float32)
        value_rows = context[:, :, :, 1, :].astype(jnp.float32)
        scores = jnp.einsum('cqhd,ckhd->chqk', query_rows, key_rows) * score_scale
        row_top = lax.optimization_barrier(jnp.max(scores, axis=-1, keepdims=True))
        weights = jnp.exp(scores - row_top)
        attn_prob = weights / lax.optimization_barrier(jnp.sum(weights, axis=-1, keepdims=True))
        prob_bf = attn_prob.astype(jnp.bfloat16)
        attended = jnp.einsum('chqk,ckhd->cqhd', prob_bf.astype(jnp.float32), value_rows).astype(jnp.bfloat16)
        row_delta = lax.optimization_barrier(jnp.sum(grad_rows * attended.astype(jnp.float32), axis=-1))
        grad_prob = jnp.einsum('cqhd,ckhd->chqk', grad_rows, value_rows)
        dscore = attn_prob * (grad_prob - jnp.transpose(row_delta, (0, 2, 1))[..., None])
        dscore_bf = dscore.astype(jnp.bfloat16).astype(jnp.float32)
        grad_query = (jnp.einsum('chqk,ckhd->cqhd', dscore_bf, key_rows) * score_scale).astype(jnp.bfloat16)
        grad_keys = (jnp.einsum('chqk,cqhd->ckhd', dscore_bf, query_rows) * score_scale).astype(jnp.bfloat16)
        grad_values = jnp.einsum('chqk,cqhd->ckhd', prob_bf.astype(jnp.float32), grad_rows).astype(jnp.bfloat16)
        block_grad = jnp.stack((grad_keys, grad_values), axis=3)
        block_grad = block_grad.reshape(GROUP_SPANS * NBRS, NBR_LEN, H // 2, 2, 2, DH)
        block_grad = jnp.transpose(block_grad, (0, 4, 3, 2, 1, 5))
        grad_store = grad_store.at[block_ids].add(block_grad.astype(jnp.float32))
        shaped_out = jnp.transpose(attended.reshape(GROUP_TOK, H // 2, 2, DH), (2, 1, 0, 3))
        shaped_grad = jnp.transpose(grad_query.reshape(GROUP_TOK, H // 2, 2, DH), (2, 1, 0, 3))
        return (grad_store, (shaped_out, shaped_grad))
    grad_store, (attn_out, d_query) = lax.scan(per_group, grad_start, (query, nbr_owner, nbr_block, d_out))
    return (attn_out, d_query, grad_store.astype(jnp.bfloat16))
```

```python
import functools
import math

import jax
import jax.numpy as jnp
from jax import lax
from jax.experimental import pallas as pl
from jax.experimental.pallas import tpu as pltpu
from jax.sharding import PartitionSpec as P

RING = 8
CAP = 6
SLOTS = 2 * CAP
ROWS = RING * SLOTS
SPAN = 64
DH = 128
SEQ = 16
INST = 64
SPANS = INST // 2
BLK = 16
UNROLL = 4
SCALE = 1.0 / math.sqrt(DH)
F32 = jnp.float32
BF16 = jnp.bfloat16

SMEM = pl.BlockSpec(memory_space=pltpu.SMEM)
VMEM = pl.BlockSpec(memory_space=pltpu.VMEM)
ANY = pl.BlockSpec(memory_space=pl.ANY)

STAT_ROWS = RING * 16
SENT = 64
R_STAT, R_BLK, R_COUNT, R_SIZE = 128, 256, 384, 512


def cost(flops, nbytes):
    return pl.CostEstimate(flops=flops, bytes_accessed=nbytes, transcendentals=0)


def send_table_kernel(place, owner, table, count):
    for o in range(RING * 2):
        count[o] = 0

    def step(i, carry):
        own = owner[i]
        rank = count[own]
        count[own] = rank + 1
        chip = own >> 1
        slot = (own & 1) * CAP + rank
        table[i] = ((chip - place[0]) & (RING - 1)) * SLOTS + slot
        table[SENT + i] = chip * 16 + slot
        return carry

    lax.fori_loop(0, INST, step, 0)


def recv_table_kernel(place, names, table, count):
    def group(d, total):
        source = (place[0] - d) & (RING - 1)
        count[0] = 0
        count[1] = 0

        def step(i, total):
            own = names[source, i]
            core = own & 1
            rank = count[core]
            mine = ((own >> 1) == place[0]).astype(jnp.int32)
            count[core] = rank + mine
            slot = core * CAP + rank
            table[total] = d * SLOTS + slot
            table[R_STAT + total] = source * 16 + slot
            table[R_BLK + total] = core * BLK + names[source, INST + i]
            return total + mine

        return lax.fori_loop(0, INST, step, total)

    total = lax.fori_loop(0, RING, group, 0)
    for u in range(UNROLL):
        table[total + u] = ROWS
        table[R_STAT + total + u] = STAT_ROWS
        table[R_BLK + total + u] = 0
    table[R_COUNT] = total


def pack_kernel(table, rows, after, *refs):
    outs, stage, sems = refs[:RING], refs[RING], refs[RING + 1]

    def step(i, carry):
        row = table[i]
        span = i >> 1
        start = pl.multiple_of((span & 1) * SPAN, SPAN)
        for kind in range(2):
            stage[row, kind] = rows[span >> 1, kind, pl.ds(start, SPAN), :]
        return carry

    lax.fori_loop(0, INST, step, 0, unroll=4)
    copies = [
        pltpu.make_async_copy(stage.at[pl.ds(d * SLOTS, SLOTS)], outs[d], sems.at[d])
        for d in range(RING)
    ]
    for copy in copies:
        copy.start()
    for copy in copies:
        copy.wait()


def load_rows(parts, stage, sems):
    copies = [
        pltpu.make_async_copy(parts[d], stage.at[pl.ds(d * SLOTS, SLOTS)], sems.at[d])
        for d in range(RING)
    ]
    for copy in copies:
        copy.start()
    return copies


def load_store(pair, core, own, other, store, sems):
    mine = pltpu.make_async_copy(
        own.at[:, :, core, pair], store.at[pl.ds(core * BLK, BLK)], sems.at[RING]
    )
    theirs = pltpu.make_async_copy(
        other.at[:, :, pair], store.at[pl.ds((1 - core) * BLK, BLK)], sems.at[RING + 1]
    )
    mine.start()
    theirs.start()
    return [mine, theirs]


def dot(a, b, dims):
    return lax.dot_general(a, b, (dims, ((), ())), preferred_element_type=F32)


NT = ((1,), (1,))
NN = ((1,), (0,))
TN = ((0,), (0,))


def stat_kernel(pair, place, table, *refs):
    parts, own, other, out, stage, store, stats, sems = (
        refs[:RING],
        *refs[RING : RING + 7],
    )
    copies = load_rows(parts, stage, sems) + load_store(pair, place[1], own, other, store, sems)
    stage[ROWS] = jnp.zeros(stage.shape[1:], BF16)
    stats[...] = jnp.zeros(stats.shape, F32)
    for copy in copies:
        copy.wait()

    def step(it, carry):
        for u in range(UNROLL):
            n = it * UNROLL + u
            row, srow, block = table[n], table[R_STAT + n], table[R_BLK + n]
            score = dot(store[block, 0], stage[row, 0], NT) * SCALE
            gprob = dot(store[block, 1], stage[row, 1], NT)
            top = jnp.max(score, axis=0, keepdims=True)
            weight = jnp.exp(score - top)
            total = jnp.sum(weight, axis=0, keepdims=True)
            delta = jnp.sum(weight * gprob, axis=0, keepdims=True) / total
            stats[pl.ds(srow, 1), :] = jnp.concatenate([top + jnp.log(total), delta], axis=1)
        return carry

    lax.fori_loop(0, (table[R_COUNT] + UNROLL - 1) // UNROLL, step, 0)
    out[...] = stats[:STAT_ROWS]


def merge_kernel(table, given, out, first, second, merged):
    def take(c, carry):
        first[pl.ds(c, 1), :] = given[pl.ds(table[SENT + 2 * c], 1), :]
        second[pl.ds(c, 1), :] = given[pl.ds(table[SENT + 2 * c + 1], 1), :]
        return carry

    lax.fori_loop(0, SPANS, take, 0, unroll=8)
    log1, log2 = first[:, :SPAN], second[:, :SPAN]
    top = jnp.maximum(log1, log2)
    both = top + jnp.log(jnp.exp(log1 - top) + jnp.exp(log2 - top))
    delta = jnp.exp(log1 - both) * first[:, SPAN:] + jnp.exp(log2 - both) * second[:, SPAN:]
    merged[...] = jnp.concatenate([both, delta], axis=1)
    out[...] = jnp.zeros(out.shape, F32)

    def put(c, carry):
        row = merged[pl.ds(c, 1), :]
        out[pl.ds(table[SENT + 2 * c], 1), :] = row
        out[pl.ds(table[SENT + 2 * c + 1], 1), :] = row
        return carry

    lax.fori_loop(0, SPANS, put, 0, unroll=8)


def grad_kernel(pair, place, table, given, *refs):
    parts, own, other = refs[:RING], refs[RING], refs[RING + 1]
    outs = refs[RING + 2 : 2 * RING + 2]
    keep, send, stage, store, stats, result, total, sems = refs[2 * RING + 2 :]
    copies = load_rows(parts, stage, sems) + load_store(pair, place[1], own, other, store, sems)
    stage[ROWS] = jnp.zeros(stage.shape[1:], BF16)
    stats[:STAT_ROWS] = given[...]
    stats[STAT_ROWS:] = jnp.zeros((8, DH), F32)

    def clear(b, carry):
        total[b] = jnp.zeros(total.shape[1:], F32)
        return carry

    lax.fori_loop(0, 2 * BLK, clear, 0)
    for copy in copies:
        copy.wait()

    def step(it, carry):
        adds = []
        for u in range(UNROLL):
            n = it * UNROLL + u
            row, srow, block = table[n], table[R_STAT + n], table[R_BLK + n]
            query, grad = stage[row, 0], stage[row, 1]
            key, value = store[block, 0], store[block, 1]
            stat = stats[pl.ds(srow, 1), :]
            score = dot(key, query, NT) * SCALE
            prob = jnp.exp(score - stat[:, :SPAN])
            dscore = (prob * (dot(value, grad, NT) - stat[:, SPAN:])).astype(BF16)
            prob = prob.astype(BF16)
            result[row, 0] = dot(prob, value, TN).astype(BF16)
            result[row, 1] = (dot(dscore, key, TN) * SCALE).astype(BF16)
            total[block, 0] += dot(dscore, query, NN)
            total[block, 1] += dot(prob, grad, NN)
        return carry

    lax.fori_loop(0, (table[R_COUNT] + UNROLL - 1) // UNROLL, step, 0)
    copies = [
        pltpu.make_async_copy(result.at[pl.ds(d * SLOTS, SLOTS)], outs[d], sems.at[d])
        for d in range(RING)
    ]
    for copy in copies:
        copy.start()

    def finish(b, carry):
        for out, core in ((keep, place[1]), (send, 1 - place[1])):
            out[b, 0] = (total[core * BLK + b, 0] * SCALE).astype(BF16)
            out[b, 1] = total[core * BLK + b, 1].astype(BF16)
        return carry

    lax.fori_loop(0, BLK, finish, 0)
    for copy in copies:
        copy.wait()


def unpack_kernel(table, *refs):
    parts, out, stage, sems = refs[:RING], *refs[RING:]
    for copy in load_rows(parts, stage, sems):
        copy.wait()

    def step(c, carry):
        one, two = table[2 * c], table[2 * c + 1]
        start = pl.multiple_of((c & 1) * SPAN, SPAN)
        for kind in range(2):
            summed = stage[one, kind].astype(F32) + stage[two, kind].astype(F32)
            out[c >> 1, kind, pl.ds(start, SPAN), :] = summed.astype(BF16)
        return carry

    lax.fori_loop(0, SPANS, step, 0, unroll=2)


def join_kernel(place, keep0, keep1, got0, got1, out, sems):
    core = place[1]
    copies = []
    for n, (ref, half, pair) in enumerate(
        ((keep0, core, 0), (keep1, core, 1), (got0, 1 - core, 0), (got1, 1 - core, 1))
    ):
        copies.append(pltpu.make_async_copy(ref, out.at[:, :, half, pair], sems.at[n]))
    for copy in copies:
        copy.start()
    for copy in copies:
        copy.wait()


def shape(dims, dtype=BF16):
    return jax.ShapeDtypeStruct(dims, dtype)


PART = (SLOTS, 2, SPAN, DH)
PARAMS = pltpu.CompilerParams(vmem_limit_bytes=40 * 1024 * 1024)
STAGE = pltpu.VMEM((ROWS + 1, 2, SPAN, DH), BF16)
STORE = pltpu.VMEM((2 * BLK, 2, 128, DH), BF16)
STATS = pltpu.VMEM((STAT_ROWS + 8, DH), F32)
SEMS = pltpu.SemaphoreType.DMA((RING + 2,))


def ring_send(parts, sign):
    got = [None] * RING
    for d in (4, 3, 5, 2, 6, 1, 7):
        pairs = [(i, (i + sign * d) % RING) for i in range(RING)]
        got[d] = lax.ppermute(parts[d], "grp", pairs)
    got[0] = parts[0]
    return got


def on_device(query, kv_store, nbr_owner, nbr_block, d_out):
    core = lax.axis_index("store")
    place = jnp.stack([lax.axis_index("grp"), core]).astype(jnp.int32)
    owner = nbr_owner.reshape(INST)
    names = jnp.concatenate([owner, nbr_block.reshape(INST)]).reshape(1, 2 * INST)
    names = lax.all_gather(names, "grp", tiled=True)
    swap = [(0, 1), (1, 0)]
    kv_other = lax.ppermute(
        lax.dynamic_index_in_dim(kv_store, 1 - core, 2, keepdims=False), "store", swap
    )

    send_table = pl.pallas_call(
        send_table_kernel,
        out_shape=shape((2 * INST,), jnp.int32),
        in_specs=[SMEM, SMEM],
        out_specs=SMEM,
        scratch_shapes=[pltpu.SMEM((2 * RING,), jnp.int32)],
        name="send_table",
    )(place, owner)
    recv_table = pl.pallas_call(
        recv_table_kernel,
        out_shape=shape((R_SIZE,), jnp.int32),
        in_specs=[SMEM, SMEM],
        out_specs=SMEM,
        scratch_shapes=[pltpu.SMEM((2,), jnp.int32)],
        name="recv_table",
    )(place, names)

    query_rows = query.reshape(SEQ, 2, 128, DH)
    grad_rows = d_out.reshape(SEQ, 2, 128, DH)

    arrived = []
    after = owner
    for pair in range(2):
        rows = jnp.stack([query_rows[:, pair], grad_rows[:, pair]], axis=1)
        rows = lax.all_to_all(rows, "seq", split_axis=0, concat_axis=0, tiled=True)
        parts = pl.pallas_call(
            pack_kernel,
            out_shape=[shape(PART)] * RING,
            in_specs=[SMEM, VMEM, ANY],
            out_specs=[ANY] * RING,
            scratch_shapes=[
                pltpu.VMEM((ROWS, 2, SPAN, DH), BF16),
                pltpu.SemaphoreType.DMA((RING,)),
            ],
            compiler_params=PARAMS,
            cost_estimate=cost(0, 8 << 20),
            name="pack",
        )(send_table, rows, after)
        got = ring_send(parts, 1)
        after = got[1]
        arrived.append(got)

    results = []
    kv_grads = []
    for pair in range(2):
        parts = arrived[pair]
        stats = pl.pallas_call(
            functools.partial(stat_kernel, pair),
            out_shape=shape((STAT_ROWS, DH), F32),
            in_specs=[SMEM, SMEM] + [ANY] * (RING + 2),
            out_specs=VMEM,
            scratch_shapes=[STAGE, STORE, STATS, SEMS],
            compiler_params=PARAMS,
            cost_estimate=cost(8 << 30, 8 << 20),
            name="stats",
        )(place, recv_table, *parts, kv_store, kv_other)
        stats = lax.all_to_all(stats, "grp", split_axis=0, concat_axis=0, tiled=True)
        stats = pl.pallas_call(
            merge_kernel,
            out_shape=shape((STAT_ROWS, DH), F32),
            in_specs=[SMEM, VMEM],
            out_specs=VMEM,
            scratch_shapes=[pltpu.VMEM((SPANS, DH), F32)] * 3,
            name="merge",
        )(send_table, stats)
        stats = lax.all_to_all(stats, "grp", split_axis=0, concat_axis=0, tiled=True)
        outs = pl.pallas_call(
            functools.partial(grad_kernel, pair),
            out_shape=[shape(PART)] * RING + [shape((BLK, 2, 128, DH))] * 2,
            in_specs=[SMEM, SMEM, VMEM] + [ANY] * (RING + 2),
            out_specs=[ANY] * RING + [VMEM, VMEM],
            scratch_shapes=[
                STAGE,
                STORE,
                STATS,
                STAGE,
                pltpu.VMEM((2 * BLK, 2, 128, DH), F32),
                SEMS,
            ],
            compiler_params=PARAMS,
            cost_estimate=cost(16 << 30, 16 << 20),
            name="grads",
        )(place, recv_table, stats, *parts, kv_store, kv_other)
        got = ring_send(outs[:RING], -1)
        kv_grads.append((outs[RING], lax.ppermute(outs[RING + 1], "store", swap)))
        rows = pl.pallas_call(
            unpack_kernel,
            out_shape=shape((SEQ, 2, 128, DH)),
            in_specs=[SMEM] + [ANY] * RING,
            out_specs=VMEM,
            scratch_shapes=[
                pltpu.VMEM((ROWS, 2, SPAN, DH), BF16),
                pltpu.SemaphoreType.DMA((RING,)),
            ],
            compiler_params=PARAMS,
            cost_estimate=cost(0, 8 << 20),
            name="unpack",
        )(send_table, *got)
        results.append(lax.all_to_all(rows, "seq", split_axis=0, concat_axis=0, tiled=True))

    d_kv = pl.pallas_call(
        join_kernel,
        out_shape=shape(kv_store.shape),
        in_specs=[SMEM] + [ANY] * 4,
        out_specs=ANY,
        scratch_shapes=[pltpu.SemaphoreType.DMA((4,))],
        cost_estimate=cost(0, 8 << 20),
        name="join",
    )(place, kv_grads[0][0], kv_grads[1][0], kv_grads[0][1], kv_grads[1][1])
    attn_out = jnp.stack([results[0][:, 0], results[1][:, 0]], axis=1).reshape(query.shape)
    d_query = jnp.stack([results[0][:, 1], results[1][:, 1]], axis=1).reshape(query.shape)
    return (attn_out, d_query, d_kv)


def solution(mesh):
    in_specs = (
        P("grp", "store", None, "seq", None),
        P(("grp", "store"), None, None, "seq", None, None),
        P("grp", None, None),
        P("grp", None, None),
        P("grp", "store", None, "seq", None),
    )
    out_specs = (
        P("grp", "store", None, "seq", None),
        P("grp", "store", None, "seq", None),
        P(("grp", "store"), None, None, "seq", None, None),
    )
    return jax.shard_map(
        on_device, mesh=mesh, in_specs=in_specs, out_specs=out_specs, check_vma=False
    )
```

```python
import functools
import math

import jax
import jax.numpy as jnp
from jax import lax
from jax.experimental import pallas as pl
from jax.experimental.pallas import tpu as pltpu
from jax.sharding import PartitionSpec as P

RING = 8
CAP = 6
SLOTS = 2 * CAP
ROWS = RING * SLOTS
SPAN = 64
DH = 128
SEQ = 16
INST = 64
SPANS = INST // 2
BLK = 16
UNROLL = 4
COST = 1 << 10
SCALE = 1.0 / math.sqrt(DH)
F32 = jnp.float32
BF16 = jnp.bfloat16

SMEM = pl.BlockSpec(memory_space=pltpu.SMEM)
VMEM = pl.BlockSpec(memory_space=pltpu.VMEM)
ANY = pl.BlockSpec(memory_space=pltpu.HBM)

STAT_ROWS = RING * 16
SENT = 64
R_STAT, R_BLK, R_COUNT, R_SIZE = 128, 256, 384, 512


def cost(flops, nbytes):
    return pl.CostEstimate(flops=flops, bytes_accessed=nbytes, transcendentals=0)


def send_table_kernel(place, owner, table, count):
    for o in range(RING * 2):
        count[o] = 0

    def step(i, carry):
        own = owner[i]
        rank = count[own]
        count[own] = rank + 1
        chip = own >> 1
        slot = (own & 1) * CAP + rank
        table[i] = ((chip - place[0]) & (RING - 1)) * SLOTS + slot
        table[SENT + i] = chip * 16 + slot
        return carry

    lax.fori_loop(0, INST, step, 0)


def recv_table_kernel(place, names, table, count):
    def group(d, total):
        source = (place[0] - d) & (RING - 1)
        count[0] = 0
        count[1] = 0

        def step(i, total):
            own = names[source, i]
            core = own & 1
            rank = count[core]
            mine = ((own >> 1) == place[0]).astype(jnp.int32)
            count[core] = rank + mine
            slot = core * CAP + rank
            table[total] = d * SLOTS + slot
            table[R_STAT + total] = source * 16 + slot
            table[R_BLK + total] = core * BLK + names[source, INST + i]
            return total + mine

        return lax.fori_loop(0, INST, step, total)

    total = lax.fori_loop(0, RING, group, 0)
    for u in range(UNROLL):
        table[total + u] = ROWS
        table[R_STAT + total + u] = STAT_ROWS
        table[R_BLK + total + u] = 0
    table[R_COUNT] = total


def pack_kernel(table, rows, after, *refs):
    outs, stage, sems = refs[:RING], refs[RING], refs[RING + 1]

    def step(i, carry):
        row = table[i]
        span = i >> 1
        start = pl.multiple_of((span & 1) * SPAN, SPAN)
        for kind in range(2):
            stage[row, kind] = rows[span >> 1, kind, pl.ds(start, SPAN), :]
        return carry

    lax.fori_loop(0, INST, step, 0, unroll=4)
    copies = [
        pltpu.make_async_copy(stage.at[pl.ds(d * SLOTS, SLOTS)], outs[d], sems.at[d])
        for d in range(RING)
    ]
    for copy in copies:
        copy.start()
    for copy in copies:
        copy.wait()


def load_rows(parts, stage, sems):
    copies = [
        pltpu.make_async_copy(parts[d], stage.at[pl.ds(d * SLOTS, SLOTS)], sems.at[d])
        for d in range(RING)
    ]
    for copy in copies:
        copy.start()
    return copies


def load_store(pair, core, own, other, store, sems):
    mine = pltpu.make_async_copy(
        own.at[:, :, core, pair], store.at[pl.ds(core * BLK, BLK)], sems.at[RING]
    )
    theirs = pltpu.make_async_copy(
        other.at[:, :, pair], store.at[pl.ds((1 - core) * BLK, BLK)], sems.at[RING + 1]
    )
    mine.start()
    theirs.start()
    return [mine, theirs]


def dot(a, b, dims):
    return lax.dot_general(a, b, (dims, ((), ())), preferred_element_type=F32)


NT = ((1,), (1,))
NN = ((1,), (0,))
TN = ((0,), (0,))


def stat_kernel(pair, place, table, *refs):
    parts, own, other, out, stage, store, stats, sems = (
        refs[:RING],
        *refs[RING : RING + 7],
    )
    copies = load_rows(parts, stage, sems) + load_store(pair, place[1], own, other, store, sems)
    stage[ROWS] = jnp.zeros(stage.shape[1:], BF16)
    stats[...] = jnp.zeros(stats.shape, F32)
    for copy in copies:
        copy.wait()

    def step(it, carry):
        for u in range(UNROLL):
            n = it * UNROLL + u
            row, srow, block = table[n], table[R_STAT + n], table[R_BLK + n]
            score = dot(store[block, 0], stage[row, 0], NT) * SCALE
            gprob = dot(store[block, 1], stage[row, 1], NT)
            top = jnp.max(score, axis=0, keepdims=True)
            weight = jnp.exp(score - top)
            total = jnp.sum(weight, axis=0, keepdims=True)
            delta = jnp.sum(weight * gprob, axis=0, keepdims=True) / total
            stats[pl.ds(srow, 1), :] = jnp.concatenate([top + jnp.log(total), delta], axis=1)
        return carry

    lax.fori_loop(0, (table[R_COUNT] + UNROLL - 1) // UNROLL, step, 0)
    out[...] = stats[:STAT_ROWS]


def merge_kernel(table, given, out, first, second, merged):
    def take(c, carry):
        first[pl.ds(c, 1), :] = given[pl.ds(table[SENT + 2 * c], 1), :]
        second[pl.ds(c, 1), :] = given[pl.ds(table[SENT + 2 * c + 1], 1), :]
        return carry

    lax.fori_loop(0, SPANS, take, 0, unroll=8)
    log1, log2 = first[:, :SPAN], second[:, :SPAN]
    top = jnp.maximum(log1, log2)
    both = top + jnp.log(jnp.exp(log1 - top) + jnp.exp(log2 - top))
    delta = jnp.exp(log1 - both) * first[:, SPAN:] + jnp.exp(log2 - both) * second[:, SPAN:]
    merged[...] = jnp.concatenate([both, delta], axis=1)
    out[...] = jnp.zeros(out.shape, F32)

    def put(c, carry):
        row = merged[pl.ds(c, 1), :]
        out[pl.ds(table[SENT + 2 * c], 1), :] = row
        out[pl.ds(table[SENT + 2 * c + 1], 1), :] = row
        return carry

    lax.fori_loop(0, SPANS, put, 0, unroll=8)


def grad_kernel(pair, place, table, given, *refs):
    parts, own, other = refs[:RING], refs[RING], refs[RING + 1]
    outs = refs[RING + 2 : 2 * RING + 2]
    keep, send, stage, store, stats, result, total, sems = refs[2 * RING + 2 :]
    copies = load_rows(parts, stage, sems) + load_store(pair, place[1], own, other, store, sems)
    stage[ROWS] = jnp.zeros(stage.shape[1:], BF16)
    stats[:STAT_ROWS] = given[...]
    stats[STAT_ROWS:] = jnp.zeros((8, DH), F32)

    def clear(b, carry):
        total[b] = jnp.zeros(total.shape[1:], F32)
        return carry

    lax.fori_loop(0, 2 * BLK, clear, 0)
    for copy in copies:
        copy.wait()

    def step(it, carry):
        adds = []
        for u in range(UNROLL):
            n = it * UNROLL + u
            row, srow, block = table[n], table[R_STAT + n], table[R_BLK + n]
            query, grad = stage[row, 0], stage[row, 1]
            key, value = store[block, 0], store[block, 1]
            stat = stats[pl.ds(srow, 1), :]
            score = dot(key, query, NT) * SCALE
            prob = jnp.exp(score - stat[:, :SPAN])
            dscore = (prob * (dot(value, grad, NT) - stat[:, SPAN:])).astype(BF16)
            prob = prob.astype(BF16)
            result[row, 0] = dot(prob, value, TN).astype(BF16)
            result[row, 1] = (dot(dscore, key, TN) * SCALE).astype(BF16)
            total[block, 0] += dot(dscore, query, NN)
            total[block, 1] += dot(prob, grad, NN)
        return carry

    lax.fori_loop(0, (table[R_COUNT] + UNROLL - 1) // UNROLL, step, 0)
    copies = [
        pltpu.make_async_copy(result.at[pl.ds(d * SLOTS, SLOTS)], outs[d], sems.at[d])
        for d in range(RING)
    ]
    for copy in copies:
        copy.start()

    def finish(b, carry):
        for out, core in ((keep, place[1]), (send, 1 - place[1])):
            out[b, 0] = (total[core * BLK + b, 0] * SCALE).astype(BF16)
            out[b, 1] = total[core * BLK + b, 1].astype(BF16)
        return carry

    lax.fori_loop(0, BLK, finish, 0)
    for copy in copies:
        copy.wait()


def unpack_kernel(table, *refs):
    parts, out, stage, sems = refs[:RING], *refs[RING:]
    for copy in load_rows(parts, stage, sems):
        copy.wait()

    def step(c, carry):
        one, two = table[2 * c], table[2 * c + 1]
        start = pl.multiple_of((c & 1) * SPAN, SPAN)
        for kind in range(2):
            summed = stage[one, kind].astype(F32) + stage[two, kind].astype(F32)
            out[c >> 1, kind, pl.ds(start, SPAN), :] = summed.astype(BF16)
        return carry

    lax.fori_loop(0, SPANS, step, 0, unroll=2)


def join_kernel(place, keep0, keep1, got0, got1, out):
    core = place[1]
    for ref, half, pair in (
        (keep0, core, 0),
        (keep1, core, 1),
        (got0, 1 - core, 0),
        (got1, 1 - core, 1),
    ):
        for kind in range(2):
            out[0, kind, half, pair] = ref[0, kind]


def shape(dims, dtype=BF16):
    return jax.ShapeDtypeStruct(dims, dtype)


PART = (SLOTS, 2, SPAN, DH)
PARAMS = pltpu.CompilerParams(vmem_limit_bytes=60 * 1024 * 1024)
STAGE = pltpu.VMEM((ROWS + 1, 2, SPAN, DH), BF16)
STORE = pltpu.VMEM((2 * BLK, 2, 128, DH), BF16)
STATS = pltpu.VMEM((STAT_ROWS + 8, DH), F32)
SEMS = pltpu.SemaphoreType.DMA((RING + 2,))


def ring_send(parts, sign):
    got = [None] * RING
    for d in (4, 3, 5, 2, 6, 1, 7):
        pairs = [(i, (i + sign * d) % RING) for i in range(RING)]
        got[d] = lax.ppermute(parts[d], "grp", pairs)
    got[0] = parts[0]
    return got


def on_device(query, kv_store, nbr_owner, nbr_block, d_out):
    core = lax.axis_index("store")
    place = jnp.stack([lax.axis_index("grp"), core]).astype(jnp.int32)
    owner = nbr_owner.reshape(INST)
    names = jnp.concatenate([owner, nbr_block.reshape(INST)]).reshape(1, 2 * INST)
    names = lax.all_gather(names, "grp", tiled=True)
    swap = [(0, 1), (1, 0)]
    kv_other = lax.ppermute(
        lax.dynamic_index_in_dim(kv_store, 1 - core, 2, keepdims=False), "store", swap
    )

    send_table = pl.pallas_call(
        send_table_kernel,
        out_shape=shape((2 * INST,), jnp.int32),
        in_specs=[SMEM, SMEM],
        out_specs=SMEM,
        scratch_shapes=[pltpu.SMEM((2 * RING,), jnp.int32)],
        name="send_table",
    )(place, owner)
    recv_table = pl.pallas_call(
        recv_table_kernel,
        out_shape=shape((R_SIZE,), jnp.int32),
        in_specs=[SMEM, SMEM],
        out_specs=SMEM,
        scratch_shapes=[pltpu.SMEM((2,), jnp.int32)],
        name="recv_table",
    )(place, names)

    query_rows = query.reshape(SEQ, 2, 128, DH)
    grad_rows = d_out.reshape(SEQ, 2, 128, DH)

    arrived = []
    after = owner
    for pair in range(2):
        rows = jnp.stack([query_rows[:, pair], grad_rows[:, pair]], axis=1)
        rows = lax.all_to_all(rows, "seq", split_axis=0, concat_axis=0, tiled=True)
        parts = pl.pallas_call(
            pack_kernel,
            out_shape=[shape(PART)] * RING,
            in_specs=[SMEM, VMEM, ANY],
            out_specs=[ANY] * RING,
            scratch_shapes=[
                pltpu.VMEM((ROWS, 2, SPAN, DH), BF16),
                pltpu.SemaphoreType.DMA((RING,)),
            ],
            compiler_params=PARAMS,
            cost_estimate=cost(0, COST),
            name="pack",
        )(send_table, rows, after)
        got = ring_send(parts, 1)
        arrived.append(got)
        after = recv_table

    results = []
    kv_grads = []
    for pair in range(2):
        parts = arrived[pair]
        stats = pl.pallas_call(
            functools.partial(stat_kernel, pair),
            out_shape=shape((STAT_ROWS, DH), F32),
            in_specs=[SMEM, SMEM] + [ANY] * (RING + 2),
            out_specs=VMEM,
            scratch_shapes=[STAGE, STORE, STATS, SEMS],
            compiler_params=PARAMS,
            cost_estimate=cost(COST, COST),
            name="stats",
        )(place, recv_table, *parts, kv_store, kv_other)
        stats = lax.all_to_all(stats, "grp", split_axis=0, concat_axis=0, tiled=True)
        stats = pl.pallas_call(
            merge_kernel,
            out_shape=shape((STAT_ROWS, DH), F32),
            in_specs=[SMEM, VMEM],
            out_specs=VMEM,
            scratch_shapes=[pltpu.VMEM((SPANS, DH), F32)] * 3,
            name="merge",
        )(send_table, stats)
        stats = lax.all_to_all(stats, "grp", split_axis=0, concat_axis=0, tiled=True)
        outs = pl.pallas_call(
            functools.partial(grad_kernel, pair),
            out_shape=[shape(PART)] * RING + [shape((BLK, 2, 128, DH))] * 2,
            in_specs=[SMEM, SMEM, VMEM] + [ANY] * (RING + 2),
            out_specs=[ANY] * RING + [VMEM, VMEM],
            scratch_shapes=[
                STAGE,
                STORE,
                STATS,
                STAGE,
                pltpu.VMEM((2 * BLK, 2, 128, DH), F32),
                SEMS,
            ],
            compiler_params=PARAMS,
            cost_estimate=cost(COST, COST),
            name="grads",
        )(place, recv_table, stats, *parts, kv_store, kv_other)
        got = ring_send(outs[:RING], -1)
        kv_grads.append((outs[RING], lax.ppermute(outs[RING + 1], "store", swap)))
        rows = pl.pallas_call(
            unpack_kernel,
            out_shape=shape((SEQ, 2, 128, DH)),
            in_specs=[SMEM] + [ANY] * RING,
            out_specs=VMEM,
            scratch_shapes=[
                pltpu.VMEM((ROWS, 2, SPAN, DH), BF16),
                pltpu.SemaphoreType.DMA((RING,)),
            ],
            compiler_params=PARAMS,
            cost_estimate=cost(0, COST),
            name="unpack",
        )(send_table, *got)
        results.append(lax.all_to_all(rows, "seq", split_axis=0, concat_axis=0, tiled=True))

    d_kv = pl.pallas_call(
        join_kernel,
        out_shape=shape(kv_store.shape),
        grid=(BLK,),
        in_specs=[SMEM] + [pl.BlockSpec((1, 2, 128, DH), lambda b: (b, 0, 0, 0))] * 4,
        out_specs=pl.BlockSpec((1, 2, 2, 2, 128, DH), lambda b: (b, 0, 0, 0, 0, 0)),
        cost_estimate=cost(0, COST),
        name="join",
    )(place, kv_grads[0][0], kv_grads[1][0], kv_grads[0][1], kv_grads[1][1])
    attn_out = jnp.stack([results[0][:, 0], results[1][:, 0]], axis=1).reshape(query.shape)
    d_query = jnp.stack([results[0][:, 1], results[1][:, 1]], axis=1).reshape(query.shape)
    return (attn_out, d_query, d_kv)


def solution(mesh):
    in_specs = (
        P("grp", "store", None, "seq", None),
        P(("grp", "store"), None, None, "seq", None, None),
        P("grp", None, None),
        P("grp", None, None),
        P("grp", "store", None, "seq", None),
    )
    out_specs = (
        P("grp", "store", None, "seq", None),
        P("grp", "store", None, "seq", None),
        P(("grp", "store"), None, None, "seq", None, None),
    )
    return jax.shard_map(
        on_device, mesh=mesh, in_specs=in_specs, out_specs=out_specs, check_vma=False
    )
```

```python
import functools
import math

import jax
import jax.numpy as jnp
from jax import lax
from jax.experimental import pallas as pl
from jax.experimental.pallas import tpu as pltpu
from jax.sharding import PartitionSpec as P

RING = 8
CAP = 6
SLOTS = 2 * CAP
ROWS = RING * SLOTS
SPAN = 64
DH = 128
SEQ = 16
INST = 64
SPANS = INST // 2
BLK = 16
UNROLL = 4
COST = 1 << 10
LIST = 104
SCALE = 1.0 / math.sqrt(DH)
F32 = jnp.float32
BF16 = jnp.bfloat16

SMEM = pl.BlockSpec(memory_space=pltpu.SMEM)
VMEM = pl.BlockSpec(memory_space=pltpu.VMEM)
ANY = pl.BlockSpec(memory_space=pltpu.HBM)

STAT_ROWS = RING * 16
R_STAT, R_BLK, R_PAIR, R_COUNT, R_SIZE = 128, 256, 384, 512, 640


def cost(flops, nbytes):
    return pl.CostEstimate(flops=flops, bytes_accessed=nbytes, transcendentals=0)


def recv_table_kernel(place, names, table, count, where):
    def rank(source, carry):
        for o in range(RING * 2):
            count[o] = 0

        def step(i, carry):
            own = names[source, i]
            slot = (own & 1) * CAP + count[own]
            count[own] = count[own] + 1
            where[source * INST + i] = (own >> 1) * STAT_ROWS + source * 16 + slot
            return carry

        return lax.fori_loop(0, INST, step, carry, unroll=8)

    lax.fori_loop(0, RING, rank, 0)

    def group(source, total):
        def step(i, total):
            own = names[source, i]
            at = where[source * INST + i]
            table[total] = ((place[0] - source) & (RING - 1)) * SLOTS + (at & 15)
            table[R_STAT + total] = at & (STAT_ROWS - 1)
            table[R_BLK + total] = (own & 1) * BLK + names[source, INST + i]
            table[R_PAIR + total] = where[source * INST + (i ^ 1)]
            return total + ((own >> 1) == place[0]).astype(jnp.int32)

        return lax.fori_loop(0, INST, step, total, unroll=8)

    total = lax.fori_loop(0, RING, group, 0)

    def pad(n, carry):
        table[n] = ROWS
        table[R_STAT + n] = STAT_ROWS
        table[R_BLK + n] = 0
        table[R_PAIR + n] = 0
        return carry

    lax.fori_loop(total, LIST, pad, 0)
    table[R_COUNT] = total


def part_copies(stage, parts, sems, load):
    copies = []
    for d in range(RING):
        rows = stage.at[pl.ds(d * SLOTS, SLOTS)]
        ends = (parts[d], rows) if load else (rows, parts[d])
        copies.append(pltpu.make_async_copy(*ends, sems.at[d]))
        copies[-1].start()
    return copies


def pack_kernel(place, names, rows, *refs):
    outs, (table, sent, stage, count, sems) = refs[-RING - 5 : -5], refs[-5:]
    for o in range(RING * 2):
        count[o] = 0

    def step(i, carry):
        own = names[i]
        chip = ((own >> 1) - place[0]) & (RING - 1)
        row = chip * SLOTS + (own & 1) * CAP + count[own]
        count[own] = count[own] + 1
        table[i] = row
        span = i >> 1
        start = pl.multiple_of((span & 1) * SPAN, SPAN)
        for kind in range(2):
            stage[row, kind] = rows[span >> 1, kind, pl.ds(start, SPAN), :]
        sent[0, i] = own
        sent[0, INST + i] = names[INST + i]
        return carry

    lax.fori_loop(0, INST, step, 0, unroll=4)
    for copy in part_copies(stage, outs, sems, False):
        copy.wait()


def gate_kernel(after, *refs):
    pass


def load_store(pair, core, own, other, store, sems):
    mine = pltpu.make_async_copy(
        own.at[:, :, core, pair], store.at[pl.ds(core * BLK, BLK)], sems.at[RING]
    )
    theirs = pltpu.make_async_copy(
        other.at[:, :, pair], store.at[pl.ds((1 - core) * BLK, BLK)], sems.at[RING + 1]
    )
    mine.start()
    theirs.start()
    return [mine, theirs]


def dot(a, b, dims):
    return lax.dot_general(a, b, (dims, ((), ())), preferred_element_type=F32)


NT = ((1,), (1,))
NN = ((1,), (0,))
TN = ((0,), (0,))


def load_all(pair, place, parts, own, other, stage, store, sems):
    copies = load_store(pair, place[1], own, other, store, sems)
    copies += part_copies(stage, parts, sems, True)
    stage[ROWS] = jnp.zeros(stage.shape[1:], BF16)
    return copies


def stat_kernel(pair, place, table, *refs):
    parts, own, other = refs[:RING], refs[RING], refs[RING + 1]
    out, stage, store, stats, sems = refs[-5:]
    copies = load_all(pair, place, parts, own, other, stage, store, sems)
    stats[...] = jnp.zeros(stats.shape, F32)
    for copy in copies:
        copy.wait()

    def step(it, carry):
        for u in range(UNROLL):
            n = it * UNROLL + u
            row, srow, block = table[n], table[R_STAT + n], table[R_BLK + n]
            score = dot(store[block, 0], stage[row, 0], NT) * SCALE
            gprob = dot(store[block, 1], stage[row, 1], NT)
            top = jnp.max(score, axis=0, keepdims=True)
            weight = jnp.exp(score - top)
            total = jnp.sum(weight, axis=0, keepdims=True)
            delta = jnp.sum(weight * gprob, axis=0, keepdims=True) / total
            stats[pl.ds(srow, 1), :] = jnp.concatenate([top + jnp.log(total), delta], axis=1)
        return carry

    lax.fori_loop(0, (table[R_COUNT] + UNROLL - 1) // UNROLL, step, 0)
    out[...] = stats[:STAT_ROWS]


def grad_kernel(pair, place, table, given, *refs):
    parts, own, other = refs[:RING], refs[RING], refs[RING + 1]
    outs = refs[RING + 2 : 2 * RING + 2]
    keep, send, stage, store, result, mine, theirs, stats, total, sems = refs[2 * RING + 2 :]
    copies = load_all(pair, place, parts, own, other, stage, store, sems)
    base = place[0] * STAT_ROWS

    def take(n, carry):
        srow = jnp.minimum(table[R_STAT + n], STAT_ROWS - 1)
        mine[pl.ds(n, 1), :] = given[pl.ds(base + srow, 1), :]
        theirs[pl.ds(n, 1), :] = given[pl.ds(table[R_PAIR + n], 1), :]
        return carry

    lax.fori_loop(0, LIST, take, 0, unroll=8)
    log1, log2 = mine[:, :SPAN], theirs[:, :SPAN]
    top = jnp.maximum(log1, log2)
    both = top + jnp.log(jnp.exp(log1 - top) + jnp.exp(log2 - top))
    delta = jnp.exp(log1 - both) * mine[:, SPAN:] + jnp.exp(log2 - both) * theirs[:, SPAN:]
    merged = jnp.concatenate([both, delta], axis=1)
    used = lax.broadcasted_iota(jnp.int32, (LIST, DH), 0) < table[R_COUNT]
    stats[...] = jnp.where(used, merged, 0.0)

    def clear(b, carry):
        total[b] = jnp.zeros(total.shape[1:], F32)
        return carry

    lax.fori_loop(0, 2 * BLK, clear, 0)
    for copy in copies:
        copy.wait()

    def step(it, carry):
        adds = []
        for u in range(UNROLL):
            n = it * UNROLL + u
            row, block = table[n], table[R_BLK + n]
            query, grad = stage[row, 0], stage[row, 1]
            key, value = store[block, 0], store[block, 1]
            stat = stats[pl.ds(n, 1), :]
            score = dot(key, query, NT) * SCALE
            prob = jnp.exp(score - stat[:, :SPAN])
            dscore = (prob * (dot(value, grad, NT) - stat[:, SPAN:])).astype(BF16)
            prob = prob.astype(BF16)
            result[row, 0] = dot(prob, value, TN).astype(BF16)
            result[row, 1] = (dot(dscore, key, TN) * SCALE).astype(BF16)
            total[block, 0] += dot(dscore, query, NN)
            total[block, 1] += dot(prob, grad, NN)
        return carry

    lax.fori_loop(0, (table[R_COUNT] + UNROLL - 1) // UNROLL, step, 0)
    copies = part_copies(result, outs, sems, False)

    def finish(b, carry):
        for half, core in ((keep, place[1]), (send, 1 - place[1])):
            half[b, 0] = (total[core * BLK + b, 0] * SCALE).astype(BF16)
            half[b, 1] = total[core * BLK + b, 1].astype(BF16)
        return carry

    lax.fori_loop(0, BLK, finish, 0)
    for copy in copies:
        copy.wait()


def unpack_kernel(table, *refs):
    parts, (out, stage, sems) = refs[:RING], refs[-3:]
    for copy in part_copies(stage, parts, sems, True):
        copy.wait()
    def step(c, carry):
        one, two = table[2 * c], table[2 * c + 1]
        start = pl.multiple_of((c & 1) * SPAN, SPAN)
        for kind in range(2):
            summed = stage[one, kind].astype(F32) + stage[two, kind].astype(F32)
            out[c >> 1, kind, pl.ds(start, SPAN), :] = summed.astype(BF16)
        return carry

    lax.fori_loop(0, SPANS, step, 0, unroll=2)


def join_kernel(place, keep0, keep1, got0, got1, out):
    core = place[1]
    for ref, half, pair in (
        (keep0, core, 0),
        (keep1, core, 1),
        (got0, 1 - core, 0),
        (got1, 1 - core, 1),
    ):
        for kind in range(2):
            out[0, kind, half, pair] = ref[0, kind]


def shape(dims, dtype=BF16):
    return jax.ShapeDtypeStruct(dims, dtype)


PARAMS = pltpu.CompilerParams(vmem_limit_bytes=60 * 1024 * 1024)
PART = (SLOTS, 2, SPAN, DH)
STAGE = pltpu.VMEM((ROWS + 1, 2, SPAN, DH), BF16)
STORE = pltpu.VMEM((2 * BLK, 2, 128, DH), BF16)
SEMS = pltpu.SemaphoreType.DMA((RING + 2,))


EARLY, LATE = (3, 5, 4, 1, 7), (2, 6)


def exchange(rows):
    return lax.all_to_all(rows, "seq", split_axis=0, concat_axis=0, tiled=True)


def ring_send(parts, sign, gated=(), after=None):
    parts = list(parts)
    if gated:
        for d, part in zip(gated, gate([parts[d] for d in gated], after)):
            parts[d] = part
    got = [parts[0]]
    for d in range(1, RING):
        pairs = [(i, (i + sign * d) % RING) for i in range(RING)]
        got.append(lax.ppermute(parts[d], "grp", pairs))
    return got


def gate(parts, after):
    return pl.pallas_call(
        gate_kernel,
        out_shape=[shape(part.shape, part.dtype) for part in parts],
        in_specs=[ANY] * (len(parts) + 1),
        out_specs=[ANY] * len(parts),
        input_output_aliases={n + 1: n for n in range(len(parts))},
        cost_estimate=cost(0, COST),
        name="gate",
    )(after, *parts)


def on_device(query, kv_store, nbr_owner, nbr_block, d_out):
    core = lax.axis_index("store")
    place = jnp.stack([lax.axis_index("grp"), core]).astype(jnp.int32)
    names = jnp.concatenate([nbr_owner.reshape(INST), nbr_block.reshape(INST)])
    swap = [(0, 1), (1, 0)]
    kv_other = lax.ppermute(
        lax.dynamic_index_in_dim(kv_store, 1 - core, 2, keepdims=False), "store", swap
    )
    query_rows = query.reshape(SEQ, 2, 128, DH)
    grad_rows = d_out.reshape(SEQ, 2, 128, DH)

    arrived = []
    after = []
    for pair in range(2):
        rows = jnp.stack([query_rows[:, pair], grad_rows[:, pair]], axis=1)
        rows = exchange(rows)
        outs = pl.pallas_call(
            pack_kernel,
            out_shape=[shape(PART)] * RING
            + [shape((INST,), jnp.int32), shape((1, 2 * INST), jnp.int32)],
            in_specs=[SMEM, SMEM, VMEM] + [ANY] * len(after),
            out_specs=[ANY] * RING + [SMEM, SMEM],
            scratch_shapes=[
                pltpu.VMEM((ROWS, 2, SPAN, DH), BF16),
                pltpu.SMEM((2 * RING,), jnp.int32),
                pltpu.SemaphoreType.DMA((RING,)),
            ],
            compiler_params=PARAMS,
            cost_estimate=cost(0, COST),
            name="pack",
        )(place, names, rows, *after)
        send_table, sent = outs[RING:]
        if pair == 0:
            recv_table = pl.pallas_call(
                recv_table_kernel,
                out_shape=shape((R_SIZE,), jnp.int32),
                in_specs=[SMEM, SMEM],
                out_specs=SMEM,
                scratch_shapes=[
                    pltpu.SMEM((2 * RING,), jnp.int32),
                    pltpu.SMEM((RING * INST,), jnp.int32),
                ],
                cost_estimate=cost(0, COST),
                name="recv_table",
            )(place, lax.all_gather(sent, "grp", tiled=True))
            arrived.append(ring_send(outs[:RING], 1, LATE, recv_table))
            after = [arrived[0][d] for d in EARLY]
        else:
            arrived.append(ring_send(outs[:RING], 1))

    partial = []
    kv_grads = []
    after = []
    for pair in range(2):
        stats = pl.pallas_call(
            functools.partial(stat_kernel, pair),
            out_shape=shape((STAT_ROWS, DH), F32),
            in_specs=[SMEM, SMEM] + [ANY] * (RING + 2 + len(after)),
            out_specs=VMEM,
            scratch_shapes=[STAGE, STORE, pltpu.VMEM((STAT_ROWS + 8, DH), F32), SEMS],
            compiler_params=PARAMS,
            cost_estimate=cost(COST, COST),
            name="stats",
        )(place, recv_table, *arrived[pair], kv_store, kv_other, *after)
        given = lax.all_gather(stats, "grp").reshape(RING * STAT_ROWS, DH)
        outs = pl.pallas_call(
            functools.partial(grad_kernel, pair),
            out_shape=[shape(PART)] * RING + [shape((BLK, 2, 128, DH))] * 2,
            in_specs=[SMEM, SMEM, VMEM] + [ANY] * (RING + 2),
            out_specs=[ANY] * RING + [VMEM] * 2,
            scratch_shapes=[STAGE, STORE, STAGE]
            + [pltpu.VMEM((LIST, DH), F32)] * 3
            + [pltpu.VMEM((2 * BLK, 2, 128, DH), F32), SEMS],
            compiler_params=PARAMS,
            cost_estimate=cost(COST, COST),
            name="grads",
        )(place, recv_table, given, *arrived[pair], kv_store, kv_other)
        partial.append(outs[:RING])
        after = [outs[RING]]
        kv_grads.append((outs[RING], lax.ppermute(outs[RING + 1], "store", swap)))

    returned = [ring_send(partial[pair], -1) for pair in range(2)]
    results = []
    for pair in range(2):
        after = [returned[1][d] for d in (3, 5, 4)] if pair == 0 else []
        rows = pl.pallas_call(
            unpack_kernel,
            out_shape=shape((SEQ, 2, 128, DH)),
            in_specs=[SMEM] + [ANY] * (RING + len(after)),
            out_specs=VMEM,
            scratch_shapes=[
                pltpu.VMEM((ROWS, 2, SPAN, DH), BF16),
                pltpu.SemaphoreType.DMA((RING,)),
            ],
            compiler_params=PARAMS,
            cost_estimate=cost(0, COST),
            name="unpack",
        )(send_table, *returned[pair], *after)
        results.append(exchange(rows))

    d_kv = pl.pallas_call(
        join_kernel,
        out_shape=shape(kv_store.shape),
        grid=(BLK,),
        in_specs=[SMEM] + [pl.BlockSpec((1, 2, 128, DH), lambda b: (b, 0, 0, 0))] * 4,
        out_specs=pl.BlockSpec((1, 2, 2, 2, 128, DH), lambda b: (b, 0, 0, 0, 0, 0)),
        cost_estimate=cost(0, COST),
        name="join",
    )(place, kv_grads[0][0], kv_grads[1][0], kv_grads[0][1], kv_grads[1][1])
    attn_out = jnp.stack([results[0][:, 0], results[1][:, 0]], axis=1).reshape(query.shape)
    d_query = jnp.stack([results[0][:, 1], results[1][:, 1]], axis=1).reshape(query.shape)
    return (attn_out, d_query, d_kv)


def solution(mesh):
    in_specs = (
        P("grp", "store", None, "seq", None),
        P(("grp", "store"), None, None, "seq", None, None),
        P("grp", None, None),
        P("grp", None, None),
        P("grp", "store", None, "seq", None),
    )
    out_specs = (
        P("grp", "store", None, "seq", None),
        P("grp", "store", None, "seq", None),
        P(("grp", "store"), None, None, "seq", None, None),
    )
    return jax.shard_map(
        on_device, mesh=mesh, in_specs=in_specs, out_specs=out_specs, check_vma=False
    )
```

```python
import functools
import math

import jax
import jax.numpy as jnp
from jax import lax
from jax.experimental import pallas as pl
from jax.experimental.pallas import tpu as pltpu
from jax.sharding import PartitionSpec as P

RING = 8
CAP = 6
SLOTS = 2 * CAP
ROWS = RING * SLOTS
SPAN = 64
DH = 128
SEQ = 16
INST = 64
SPANS = INST // 2
BLK = 16
UNROLL = 4
COST = 1 << 10
LIST = 104
SCALE = 1.0 / math.sqrt(DH)
F32 = jnp.float32
BF16 = jnp.bfloat16

SMEM = pl.BlockSpec(memory_space=pltpu.SMEM)
VMEM = pl.BlockSpec(memory_space=pltpu.VMEM)
ANY = pl.BlockSpec(memory_space=pltpu.HBM)

STAT_ROWS = ROWS
R_STAT, R_BLK, R_PAIR, R_COUNT, R_SIZE = 128, 256, 384, 512, 640


def cost(flops, nbytes):
    return pl.CostEstimate(flops=flops, bytes_accessed=nbytes, transcendentals=0)


def recv_table_kernel(place, names, table, count, where):
    def rank(source, carry):
        for o in range(RING * 2):
            count[o] = 0

        def step(i, carry):
            own = names[source, i]
            slot = (own & 1) * CAP + count[own]
            count[own] = count[own] + 1
            where[source * INST + i] = (own >> 1) * STAT_ROWS + source * SLOTS + slot
            return carry

        return lax.fori_loop(0, INST, step, carry, unroll=8)

    lax.fori_loop(0, RING, rank, 0)

    def group(source, total):
        def step(i, total):
            own = names[source, i]
            at = where[source * INST + i]
            local = at - (own >> 1) * STAT_ROWS
            table[total] = local + (((place[0] - source) & (RING - 1)) - source) * SLOTS
            table[R_STAT + total] = local
            table[R_BLK + total] = (own & 1) * BLK + names[source, INST + i]
            table[R_PAIR + total] = where[source * INST + (i ^ 1)]
            return total + ((own >> 1) == place[0]).astype(jnp.int32)

        return lax.fori_loop(0, INST, step, total, unroll=8)

    total = lax.fori_loop(0, RING, group, 0)

    def pad(n, carry):
        table[n] = ROWS
        table[R_STAT + n] = STAT_ROWS
        table[R_BLK + n] = 0
        table[R_PAIR + n] = 0
        return carry

    lax.fori_loop(total, LIST, pad, 0)
    table[R_COUNT] = total


def part_copies(stage, parts, sems, load):
    copies = []
    for n in range(RING):
        d = ORDER[n] if load else n
        rows = stage.at[pl.ds(d * SLOTS, SLOTS)]
        ends = (parts[n], rows) if load else (rows, parts[n])
        copies.append(pltpu.make_async_copy(*ends, sems.at[n]))
        copies[-1].start()
    return copies


def pack_kernel(place, names, rows, *refs):
    outs, (table, stage, count, sems) = refs[-RING - 4 : -4], refs[-4:]
    for o in range(RING * 2):
        count[o] = 0

    def step(i, carry):
        own = names[i]
        chip = ((own >> 1) - place[0]) & (RING - 1)
        row = chip * SLOTS + (own & 1) * CAP + count[own]
        count[own] = count[own] + 1
        table[i] = row
        span = i >> 1
        start = pl.multiple_of((span & 1) * SPAN, SPAN)
        for kind in range(2):
            stage[row, kind] = rows[span >> 1, kind, pl.ds(start, SPAN), :]
        return carry

    lax.fori_loop(0, INST, step, 0, unroll=4)
    for copy in part_copies(stage, outs, sems, False):
        copy.wait()


def gate_kernel(*refs):
    pass


def load_store(pair, core, own, other, store, sems):
    mine = pltpu.make_async_copy(
        own.at[:, :, core, pair], store.at[pl.ds(core * BLK, BLK)], sems.at[RING]
    )
    theirs = pltpu.make_async_copy(
        other.at[:, :, pair], store.at[pl.ds((1 - core) * BLK, BLK)], sems.at[RING + 1]
    )
    mine.start()
    theirs.start()
    return [mine, theirs]


def dot(a, b, dims):
    return lax.dot_general(a, b, (dims, ((), ())), preferred_element_type=F32)


NT = ((1,), (1,))
NN = ((1,), (0,))
TN = ((0,), (0,))


def load_all(pair, place, parts, own, other, stage, store, sems):
    copies = load_store(pair, place[1], own, other, store, sems)
    copies += part_copies(stage, parts, sems, True)
    stage[ROWS] = jnp.zeros(stage.shape[1:], BF16)
    return copies


def stat_kernel(pair, place, table, *refs):
    parts, own, other = refs[:RING], refs[RING], refs[RING + 1]
    out, stage, store, stats, sems = refs[-5:]
    copies = load_all(pair, place, parts, own, other, stage, store, sems)
    stats[...] = jnp.zeros(stats.shape, F32)
    for copy in copies:
        copy.wait()

    def step(it, carry):
        for u in range(UNROLL):
            n = it * UNROLL + u
            row, srow, block = table[n], table[R_STAT + n], table[R_BLK + n]
            score = dot(store[block, 0], stage[row, 0], NT) * SCALE
            gprob = dot(store[block, 1], stage[row, 1], NT)
            top = jnp.max(score, axis=0, keepdims=True)
            weight = jnp.exp(score - top)
            total = jnp.sum(weight, axis=0, keepdims=True)
            delta = jnp.sum(weight * gprob, axis=0, keepdims=True) / total
            stats[pl.ds(srow, 1), :] = jnp.concatenate([top + jnp.log(total), delta], axis=1)
        return carry

    lax.fori_loop(0, (table[R_COUNT] + UNROLL - 1) // UNROLL, step, 0)
    for chip in range(RING):
        out[pl.ds(chip * STAT_ROWS, STAT_ROWS), :] = stats[:STAT_ROWS]


def grad_kernel(pair, place, table, given, *refs):
    parts, own, other = refs[:RING], refs[RING], refs[RING + 1]
    outs = refs[-RING - 10 : -10]
    keep, send, stage, store, result, mine, theirs, stats, total, sems = refs[-10:]
    copies = load_all(pair, place, parts, own, other, stage, store, sems)
    base = place[0] * STAT_ROWS

    def take(n, carry):
        srow = jnp.minimum(table[R_STAT + n], STAT_ROWS - 1)
        mine[pl.ds(n, 1), :] = given[pl.ds(base + srow, 1), :]
        theirs[pl.ds(n, 1), :] = given[pl.ds(table[R_PAIR + n], 1), :]
        return carry

    lax.fori_loop(0, LIST, take, 0, unroll=8)
    log1, log2 = mine[:, :SPAN], theirs[:, :SPAN]
    top = jnp.maximum(log1, log2)
    both = top + jnp.log(jnp.exp(log1 - top) + jnp.exp(log2 - top))
    delta = jnp.exp(log1 - both) * mine[:, SPAN:] + jnp.exp(log2 - both) * theirs[:, SPAN:]
    merged = jnp.concatenate([both, delta], axis=1)
    used = lax.broadcasted_iota(jnp.int32, (LIST, DH), 0) < table[R_COUNT]
    stats[...] = jnp.where(used, merged, 0.0)

    def clear(b, carry):
        total[b] = jnp.zeros(total.shape[1:], F32)
        return carry

    lax.fori_loop(0, 2 * BLK, clear, 0)
    for copy in copies:
        copy.wait()

    def step(it, carry):
        adds = []
        for u in range(UNROLL):
            n = it * UNROLL + u
            row, block = table[n], table[R_BLK + n]
            query, grad = stage[row, 0], stage[row, 1]
            key, value = store[block, 0], store[block, 1]
            stat = stats[pl.ds(n, 1), :]
            score = dot(key, query, NT) * SCALE
            prob = jnp.exp(score - stat[:, :SPAN])
            dscore = (prob * (dot(value, grad, NT) - stat[:, SPAN:])).astype(BF16)
            prob = prob.astype(BF16)
            result[row, 0] = dot(prob, value, TN).astype(BF16)
            result[row, 1] = (dot(dscore, key, TN) * SCALE).astype(BF16)
            total[block, 0] += dot(dscore, query, NN)
            total[block, 1] += dot(prob, grad, NN)
        return carry

    lax.fori_loop(0, (table[R_COUNT] + UNROLL - 1) // UNROLL, step, 0)
    copies = part_copies(result, outs, sems, False)

    def finish(b, carry):
        for half, core in ((keep, place[1]), (send, 1 - place[1])):
            half[b, 0] = (total[core * BLK + b, 0] * SCALE).astype(BF16)
            half[b, 1] = total[core * BLK + b, 1].astype(BF16)
        return carry

    lax.fori_loop(0, BLK, finish, 0)
    for copy in copies:
        copy.wait()


def unpack_kernel(table, *refs):
    parts, (out, stage, sems) = refs[:RING], refs[-3:]
    for copy in part_copies(stage, parts, sems, True):
        copy.wait()
    def step(c, carry):
        one, two = table[2 * c], table[2 * c + 1]
        start = pl.multiple_of((c & 1) * SPAN, SPAN)
        for kind in range(2):
            summed = stage[one, kind].astype(F32) + stage[two, kind].astype(F32)
            out[c >> 1, kind, pl.ds(start, SPAN), :] = summed.astype(BF16)
        return carry

    lax.fori_loop(0, SPANS, step, 0, unroll=2)


def join_kernel(place, keep0, keep1, got0, got1, out):
    core = place[1]
    for ref, half, pair in (
        (keep0, core, 0),
        (keep1, core, 1),
        (got0, 1 - core, 0),
        (got1, 1 - core, 1),
    ):
        for kind in range(2):
            out[0, kind, half, pair] = ref[0, kind]


def shape(dims, dtype=BF16):
    return jax.ShapeDtypeStruct(dims, dtype)


PARAMS = pltpu.CompilerParams(vmem_limit_bytes=60 * 1024 * 1024)
PART = (SLOTS, 2, SPAN, DH)
STAGE = pltpu.VMEM((ROWS + 1, 2, SPAN, DH), BF16)
STORE = pltpu.VMEM((2 * BLK, 2, 128, DH), BF16)
SEMS = pltpu.SemaphoreType.DMA((RING + 2,))


EARLY, LATE = (3, 5, 4, 1, 7), (2, 6)
ORDER = (0, 4, 3, 5, 2, 6, 1, 7)


def exchange(rows, axis):
    return lax.all_to_all(rows, axis, split_axis=0, concat_axis=0, tiled=True)


def ring_send(parts, sign, gated=(), after=()):
    parts = list(parts)
    if gated:
        for d, part in zip(gated, gate([parts[d] for d in gated], after)):
            parts[d] = part
    got = list(parts)
    for d in sorted(range(1, RING), key=ORDER.index):
        pairs = [(i, (i + sign * d) % RING) for i in range(RING)]
        got[d] = lax.ppermute(parts[d], "grp", pairs)
    return got


def ordered(parts):
    return [parts[d] for d in ORDER]


def gate(parts, after):
    return pl.pallas_call(
        gate_kernel,
        out_shape=[shape(part.shape, part.dtype) for part in parts],
        in_specs=[ANY] * (len(parts) + len(after)),
        out_specs=[ANY] * len(parts),
        input_output_aliases={n + len(after): n for n in range(len(parts))},
        cost_estimate=cost(0, COST),
        name="gate",
    )(*after, *parts)


def on_device(query, kv_store, nbr_owner, nbr_block, d_out):
    core = lax.axis_index("store")
    place = jnp.stack([lax.axis_index("grp"), core]).astype(jnp.int32)
    names = jnp.concatenate([nbr_owner.reshape(INST), nbr_block.reshape(INST)])
    swap = [(0, 1), (1, 0)]
    kv_other = lax.ppermute(
        lax.dynamic_index_in_dim(kv_store, 1 - core, 2, keepdims=False), "store", swap
    )
    query_rows = query.reshape(SEQ, 2, 128, DH)
    grad_rows = d_out.reshape(SEQ, 2, 128, DH)

    arrived = []
    all_names = lax.all_gather(names.reshape(1, 2 * INST), "grp", tiled=True)
    after = [kv_other, all_names]
    for pair in range(2):
        rows = jnp.stack([query_rows[:, pair], grad_rows[:, pair]], axis=1)
        if pair == 1:
            (rows,) = gate([rows], [recv_table] + after)
        rows = exchange(rows, "seq")
        outs = pl.pallas_call(
            pack_kernel,
            out_shape=[shape(PART)] * RING
            + [shape((INST,), jnp.int32)],
            in_specs=[SMEM, SMEM, VMEM] + [ANY] * len(after),
            out_specs=[ANY] * RING + [SMEM],
            scratch_shapes=[
                pltpu.VMEM((ROWS, 2, SPAN, DH), BF16),
                pltpu.SMEM((2 * RING,), jnp.int32),
                pltpu.SemaphoreType.DMA((RING,)),
            ],
            compiler_params=PARAMS,
            cost_estimate=cost(0, COST),
            name="pack",
        )(place, names, rows, *after)
        send_table = outs[RING]
        if pair == 0:
            recv_table = pl.pallas_call(
                recv_table_kernel,
                out_shape=shape((R_SIZE,), jnp.int32),
                in_specs=[SMEM, SMEM],
                out_specs=SMEM,
                scratch_shapes=[
                    pltpu.SMEM((2 * RING,), jnp.int32),
                    pltpu.SMEM((RING * INST,), jnp.int32),
                ],
                cost_estimate=cost(0, COST),
                name="recv_table",
            )(place, all_names)
            arrived.append(ring_send(outs[:RING], 1, LATE, [recv_table]))
            after = [arrived[0][d] for d in EARLY]
    bulk = outs[:RING]

    after = [send_table]
    kv_grads = []
    returned = []
    for pair in range(2):
        stats = pl.pallas_call(
            functools.partial(stat_kernel, pair),
            out_shape=shape((RING * STAT_ROWS, DH), F32),
            in_specs=[SMEM, SMEM] + [ANY] * (RING + 2 + len(after)),
            out_specs=VMEM,
            scratch_shapes=[STAGE, STORE, pltpu.VMEM((STAT_ROWS + 8, DH), F32), SEMS],
            compiler_params=PARAMS,
            cost_estimate=cost(COST, COST),
            name="stats",
        )(place, recv_table, *ordered(arrived[pair]), kv_store, kv_other, *after)
        given = exchange(stats, "grp")
        moved = ring_send(bulk, 1 - 2 * pair, range(1, RING), [stats])
        if pair == 0:
            arrived.append(moved)
        else:
            returned.append(moved)
        outs = pl.pallas_call(
            functools.partial(grad_kernel, pair),
            out_shape=[shape(PART)] * RING + [shape((BLK, 2, 128, DH))] * 2,
            in_specs=[SMEM, SMEM, VMEM] + [ANY] * (RING + 2),
            out_specs=[ANY] * RING + [VMEM] * 2,
            scratch_shapes=[STAGE, STORE, STAGE]
            + [pltpu.VMEM((LIST, DH), F32)] * 3
            + [pltpu.VMEM((2 * BLK, 2, 128, DH), F32), SEMS],
            compiler_params=PARAMS,
            cost_estimate=cost(COST, COST),
            name="grads",
        )(place, recv_table, given, *ordered(arrived[pair]), kv_store, kv_other)
        bulk = outs[:RING]
        after = [outs[RING]]
        kv_grads.append((outs[RING], lax.ppermute(outs[RING + 1], "store", swap)))
    returned.append(ring_send(bulk, -1))

    results = []
    for pair in range(2):
        rows = pl.pallas_call(
            unpack_kernel,
            out_shape=shape((SEQ, 2, 128, DH)),
            in_specs=[SMEM] + [ANY] * (RING + 1),
            out_specs=VMEM,
            scratch_shapes=[
                pltpu.VMEM((ROWS, 2, SPAN, DH), BF16),
                pltpu.SemaphoreType.DMA((RING,)),
            ],
            compiler_params=PARAMS,
            cost_estimate=cost(0, COST),
            name="unpack",
        )(send_table, *ordered(returned[pair]), kv_grads[1][0])
        results.append(exchange(rows, "seq"))

    d_kv = pl.pallas_call(
        join_kernel,
        out_shape=shape(kv_store.shape),
        grid=(BLK,),
        in_specs=[SMEM] + [pl.BlockSpec((1, 2, 128, DH), lambda b: (b, 0, 0, 0))] * 4,
        out_specs=pl.BlockSpec((1, 2, 2, 2, 128, DH), lambda b: (b, 0, 0, 0, 0, 0)),
        cost_estimate=cost(0, COST),
        name="join",
    )(place, kv_grads[0][0], kv_grads[1][0], kv_grads[0][1], kv_grads[1][1])
    attn_out = jnp.stack([results[0][:, 0], results[1][:, 0]], axis=1).reshape(query.shape)
    d_query = jnp.stack([results[0][:, 1], results[1][:, 1]], axis=1).reshape(query.shape)
    return (attn_out, d_query, d_kv)


def solution(mesh):
    in_specs = (
        P("grp", "store", None, "seq", None),
        P(("grp", "store"), None, None, "seq", None, None),
        P("grp", None, None),
        P("grp", None, None),
        P("grp", "store", None, "seq", None),
    )
    out_specs = (
        P("grp", "store", None, "seq", None),
        P("grp", "store", None, "seq", None),
        P(("grp", "store"), None, None, "seq", None, None),
    )
    return jax.shard_map(
        on_device, mesh=mesh, in_specs=in_specs, out_specs=out_specs, check_vma=False
    )
```

```python
import functools
import math

import jax
import jax.numpy as jnp
from jax import lax
from jax.experimental import pallas as pl
from jax.experimental.pallas import tpu as pltpu
from jax.sharding import PartitionSpec as P

RING = 8
CAP = 6
SLOTS = 2 * CAP
ROWS = RING * SLOTS
SPAN = 64
DH = 128
SEQ = 16
INST = 64
SPANS = INST // 2
BLK = 16
UNROLL = 4
UNROLL_STATS = 8
COST = 1 << 10
LIST = 104
SCALE = 1.0 / math.sqrt(DH)
F32 = jnp.float32
BF16 = jnp.bfloat16

SMEM = pl.BlockSpec(memory_space=pltpu.SMEM)
VMEM = pl.BlockSpec(memory_space=pltpu.VMEM)
ANY = pl.BlockSpec(memory_space=pltpu.HBM)

STAT_ROWS = ROWS
R_STAT, R_BLK, R_PAIR, R_COUNT, R_SIZE = 128, 256, 384, 512, 640


def cost(flops, nbytes):
    return pl.CostEstimate(flops=flops, bytes_accessed=nbytes, transcendentals=0)


def recv_table_kernel(place, names, table, count, where):
    def rank(source, carry):
        for o in range(RING * 2):
            count[o] = 0

        def step(i, carry):
            own = names[source, i]
            slot = (own & 1) * CAP + count[own]
            count[own] = count[own] + 1
            where[source * INST + i] = (own >> 1) * STAT_ROWS + source * SLOTS + slot
            return carry

        return lax.fori_loop(0, INST, step, carry, unroll=8)

    lax.fori_loop(0, RING, rank, 0)

    def group(source, total):
        def step(i, total):
            own = names[source, i]
            at = where[source * INST + i]
            local = at - (own >> 1) * STAT_ROWS
            table[total] = local + (((place[0] - source) & (RING - 1)) - source) * SLOTS
            table[R_STAT + total] = local
            table[R_BLK + total] = (own & 1) * BLK + names[source, INST + i]
            table[R_PAIR + total] = where[source * INST + (i ^ 1)]
            return total + ((own >> 1) == place[0]).astype(jnp.int32)

        return lax.fori_loop(0, INST, step, total, unroll=8)

    total = lax.fori_loop(0, RING, group, 0)

    def pad(n, carry):
        table[n] = ROWS
        table[R_STAT + n] = STAT_ROWS
        table[R_BLK + n] = 0
        table[R_PAIR + n] = 0
        return carry

    lax.fori_loop(total, LIST, pad, 0)
    table[R_COUNT] = total


def part_copies(stage, parts, sems, load):
    copies = []
    for n in range(RING):
        d = ORDER[n] if load else n
        rows = stage.at[pl.ds(d * SLOTS, SLOTS)]
        ends = (parts[n], rows) if load else (rows, parts[n])
        copies.append(pltpu.make_async_copy(*ends, sems.at[n]))
        copies[-1].start()
    return copies


def pack_kernel(place, names, rows, *refs):
    outs, (table, stage, count, sems) = refs[-RING - 4 : -4], refs[-4:]
    for o in range(RING * 2):
        count[o] = 0

    def step(i, carry):
        own = names[i]
        chip = ((own >> 1) - place[0]) & (RING - 1)
        row = chip * SLOTS + (own & 1) * CAP + count[own]
        count[own] = count[own] + 1
        table[i] = row
        span = i >> 1
        start = pl.multiple_of((span & 1) * SPAN, SPAN)
        for kind in range(2):
            stage[row, kind] = rows[span >> 1, kind, pl.ds(start, SPAN), :]
        return carry

    lax.fori_loop(0, INST, step, 0, unroll=4)
    for copy in part_copies(stage, outs, sems, False):
        copy.wait()


def gate_kernel(*refs):
    pass


def load_store(pair, core, own, other, store, sems):
    mine = pltpu.make_async_copy(
        own.at[:, :, core, pair], store.at[pl.ds(core * BLK, BLK)], sems.at[RING]
    )
    theirs = pltpu.make_async_copy(
        other.at[:, :, pair], store.at[pl.ds((1 - core) * BLK, BLK)], sems.at[RING + 1]
    )
    mine.start()
    theirs.start()
    return [mine, theirs]


def dot(a, b, dims):
    return lax.dot_general(a, b, (dims, ((), ())), preferred_element_type=F32)


NT = ((1,), (1,))
NN = ((1,), (0,))
TN = ((0,), (0,))


def load_all(pair, place, parts, own, other, stage, store, sems):
    copies = load_store(pair, place[1], own, other, store, sems)
    copies += part_copies(stage, parts, sems, True)
    stage[ROWS] = jnp.zeros(stage.shape[1:], BF16)
    return copies


def stat_kernel(pair, place, table, *refs):
    parts, own, other = refs[:RING], refs[RING], refs[RING + 1]
    out, stage, store, stats, sems = refs[-5:]
    copies = load_all(pair, place, parts, own, other, stage, store, sems)
    stats[...] = jnp.zeros(stats.shape, F32)
    for copy in copies:
        copy.wait()

    def step(it, carry):
        for u in range(UNROLL_STATS):
            n = it * UNROLL_STATS + u
            row, srow, block = table[n], table[R_STAT + n], table[R_BLK + n]
            score = dot(store[block, 0], stage[row, 0], NT) * SCALE
            gprob = dot(store[block, 1], stage[row, 1], NT)
            top = jnp.max(score, axis=0, keepdims=True)
            weight = jnp.exp(score - top)
            total = jnp.sum(weight, axis=0, keepdims=True)
            delta = jnp.sum(weight * gprob, axis=0, keepdims=True) / total
            stats[pl.ds(srow, 1), :] = jnp.concatenate([top + jnp.log(total), delta], axis=1)
        return carry

    lax.fori_loop(0, (table[R_COUNT] + UNROLL_STATS - 1) // UNROLL_STATS, step, 0)
    for chip in range(RING):
        out[pl.ds(chip * STAT_ROWS, STAT_ROWS), :] = stats[:STAT_ROWS]


def grad_kernel(pair, place, table, given, *refs):
    parts, own, other = refs[:RING], refs[RING], refs[RING + 1]
    outs = refs[-RING - 10 : -10]
    keep, send, stage, store, result, mine, theirs, stats, total, sems = refs[-10:]
    copies = load_all(pair, place, parts, own, other, stage, store, sems)
    base = place[0] * STAT_ROWS

    def take(n, carry):
        srow = jnp.minimum(table[R_STAT + n], STAT_ROWS - 1)
        mine[pl.ds(n, 1), :] = given[pl.ds(base + srow, 1), :]
        theirs[pl.ds(n, 1), :] = given[pl.ds(table[R_PAIR + n], 1), :]
        return carry

    lax.fori_loop(0, LIST, take, 0, unroll=8)
    log1, log2 = mine[:, :SPAN], theirs[:, :SPAN]
    top = jnp.maximum(log1, log2)
    both = top + jnp.log(jnp.exp(log1 - top) + jnp.exp(log2 - top))
    delta = jnp.exp(log1 - both) * mine[:, SPAN:] + jnp.exp(log2 - both) * theirs[:, SPAN:]
    merged = jnp.concatenate([both, delta], axis=1)
    used = lax.broadcasted_iota(jnp.int32, (LIST, DH), 0) < table[R_COUNT]
    stats[...] = jnp.where(used, merged, 0.0)

    def clear(b, carry):
        total[b] = jnp.zeros(total.shape[1:], F32)
        return carry

    lax.fori_loop(0, 2 * BLK, clear, 0)
    for copy in copies:
        copy.wait()

    def step(it, carry):
        adds = []
        for u in range(UNROLL):
            n = it * UNROLL + u
            row, block = table[n], table[R_BLK + n]
            query, grad = stage[row, 0], stage[row, 1]
            key, value = store[block, 0], store[block, 1]
            stat = stats[pl.ds(n, 1), :]
            score = dot(key, query, NT) * SCALE
            prob = jnp.exp(score - stat[:, :SPAN])
            dscore = (prob * (dot(value, grad, NT) - stat[:, SPAN:])).astype(BF16)
            prob = prob.astype(BF16)
            result[row, 0] = dot(prob, value, TN).astype(BF16)
            result[row, 1] = (dot(dscore, key, TN) * SCALE).astype(BF16)
            total[block, 0] += dot(dscore, query, NN)
            total[block, 1] += dot(prob, grad, NN)
        return carry

    lax.fori_loop(0, (table[R_COUNT] + UNROLL - 1) // UNROLL, step, 0)
    copies = part_copies(result, outs, sems, False)

    def finish(b, carry):
        for half, core in ((keep, place[1]), (send, 1 - place[1])):
            half[b, 0] = (total[core * BLK + b, 0] * SCALE).astype(BF16)
            half[b, 1] = total[core * BLK + b, 1].astype(BF16)
        return carry

    lax.fori_loop(0, BLK, finish, 0)
    for copy in copies:
        copy.wait()


def unpack_kernel(table, *refs):
    parts, (out, stage, sems) = refs[:RING], refs[-3:]
    for copy in part_copies(stage, parts, sems, True):
        copy.wait()
    def step(c, carry):
        one, two = table[2 * c], table[2 * c + 1]
        start = pl.multiple_of((c & 1) * SPAN, SPAN)
        for kind in range(2):
            summed = stage[one, kind].astype(F32) + stage[two, kind].astype(F32)
            out[c >> 1, kind, pl.ds(start, SPAN), :] = summed.astype(BF16)
        return carry

    lax.fori_loop(0, SPANS, step, 0, unroll=2)


def join_kernel(place, keep0, keep1, got0, got1, out):
    core = place[1]
    for ref, half, pair in (
        (keep0, core, 0),
        (keep1, core, 1),
        (got0, 1 - core, 0),
        (got1, 1 - core, 1),
    ):
        for kind in range(2):
            out[0, kind, half, pair] = ref[0, kind]


def shape(dims, dtype=BF16):
    return jax.ShapeDtypeStruct(dims, dtype)


PARAMS = pltpu.CompilerParams(vmem_limit_bytes=60 * 1024 * 1024)
PART = (SLOTS, 2, SPAN, DH)
STAGE = pltpu.VMEM((ROWS + 1, 2, SPAN, DH), BF16)
STORE = pltpu.VMEM((2 * BLK, 2, 128, DH), BF16)
SEMS = pltpu.SemaphoreType.DMA((RING + 2,))


EARLY = (4, 3, 5, 2, 6)
LIGHT, HEAVY = (2, 6, 1, 7), (4, 3, 5)
ORDER = (0, 4, 3, 5, 2, 6, 1, 7)


def exchange(rows, axis):
    return lax.all_to_all(rows, axis, split_axis=0, concat_axis=0, tiled=True)


def ring_send(parts, sign):
    got = list(parts)
    for d in sorted(range(1, RING), key=ORDER.index):
        pairs = [(i, (i + sign * d) % RING) for i in range(RING)]
        got[d] = lax.ppermute(parts[d], "grp", pairs)
    return got


def ordered(parts):
    return [parts[d] for d in ORDER]


def gate(parts, after):
    return pl.pallas_call(
        gate_kernel,
        out_shape=[shape(part.shape, part.dtype) for part in parts],
        in_specs=[ANY] * (len(parts) + len(after)),
        out_specs=[ANY] * len(parts),
        input_output_aliases={n + len(after): n for n in range(len(parts))},
        cost_estimate=cost(0, COST),
        name="gate",
    )(*after, *parts)


def on_device(query, kv_store, nbr_owner, nbr_block, d_out):
    core = lax.axis_index("store")
    place = jnp.stack([lax.axis_index("grp"), core]).astype(jnp.int32)
    names = jnp.concatenate([nbr_owner.reshape(INST), nbr_block.reshape(INST)])
    swap = [(0, 1), (1, 0)]
    query_rows = query.reshape(SEQ, 2, 128, DH)
    grad_rows = d_out.reshape(SEQ, 2, 128, DH)
    first = jnp.stack([query_rows[:, 0], grad_rows[:, 0]], axis=1)
    first, half = lax.optimization_barrier((first, 1 - core))
    kv_other = lax.ppermute(
        lax.dynamic_index_in_dim(kv_store, half, 2, keepdims=False), "store", swap
    )

    arrived = []
    all_names = lax.all_gather(names.reshape(1, 2 * INST), "grp", tiled=True)
    after = [kv_other, all_names]
    for pair in range(2):
        rows = first if pair == 0 else jnp.stack([query_rows[:, 1], grad_rows[:, 1]], axis=1)
        rows = exchange(rows, "seq")
        outs = pl.pallas_call(
            pack_kernel,
            out_shape=[shape(PART)] * RING
            + [shape((INST,), jnp.int32)],
            in_specs=[SMEM, SMEM, VMEM] + [ANY] * len(after),
            out_specs=[ANY] * RING + [SMEM],
            scratch_shapes=[
                pltpu.VMEM((ROWS, 2, SPAN, DH), BF16),
                pltpu.SMEM((2 * RING,), jnp.int32),
                pltpu.SemaphoreType.DMA((RING,)),
            ],
            compiler_params=PARAMS,
            cost_estimate=cost(0, COST),
            name="pack",
        )(place, names, rows, *after)
        send_table = outs[RING]
        if pair == 0:
            recv_table = pl.pallas_call(
                recv_table_kernel,
                out_shape=shape((R_SIZE,), jnp.int32),
                in_specs=[SMEM, SMEM],
                out_specs=SMEM,
                scratch_shapes=[
                    pltpu.SMEM((2 * RING,), jnp.int32),
                    pltpu.SMEM((RING * INST,), jnp.int32),
                ],
                cost_estimate=cost(0, COST),
                name="recv_table",
            )(place, all_names)
            arrived.append(ring_send(outs[:RING], 1))
            after = [recv_table] + [arrived[0][d] for d in EARLY]
    bulk = outs[:RING]

    after = [send_table]
    kv_grads = []
    returned = []
    for pair in range(2):
        stats = pl.pallas_call(
            functools.partial(stat_kernel, pair),
            out_shape=shape((RING * STAT_ROWS, DH), F32),
            in_specs=[SMEM, SMEM] + [ANY] * (RING + 2 + len(after)),
            out_specs=VMEM,
            scratch_shapes=[STAGE, STORE, pltpu.VMEM((STAT_ROWS + 8, DH), F32), SEMS],
            compiler_params=PARAMS,
            cost_estimate=cost(COST, COST),
            name="stats",
        )(place, recv_table, *ordered(arrived[pair]), kv_store, kv_other, *after)
        given = exchange(stats, "grp")
        bulk = list(bulk)
        for some, ready in ((LIGHT, stats), (HEAVY, given)):
            for d, part in zip(some, gate([bulk[d] for d in some], [ready])):
                bulk[d] = part
        moved = ring_send(bulk, 1 - 2 * pair)
        if pair == 0:
            arrived.append(moved)
        else:
            returned.append(moved)
        outs = pl.pallas_call(
            functools.partial(grad_kernel, pair),
            out_shape=[shape(PART)] * RING + [shape((BLK, 2, 128, DH))] * 2,
            in_specs=[SMEM, SMEM, VMEM] + [ANY] * (RING + 2 + len(LIGHT)),
            out_specs=[ANY] * RING + [VMEM] * 2,
            scratch_shapes=[STAGE, STORE, STAGE]
            + [pltpu.VMEM((LIST, DH), F32)] * 3
            + [pltpu.VMEM((2 * BLK, 2, 128, DH), F32), SEMS],
            compiler_params=PARAMS,
            cost_estimate=cost(COST, COST),
            name="grads",
        )(
            place,
            recv_table,
            given,
            *ordered(arrived[pair]),
            kv_store,
            kv_other,
            *(moved[d] for d in LIGHT),
        )
        bulk = outs[:RING]
        after = [outs[RING]]
        kv_grads.append((outs[RING], lax.ppermute(outs[RING + 1], "store", swap)))
    later = [returned[0][d] for d in LIGHT + HEAVY[:1]]
    returned.append(ring_send([bulk[0], *gate(bulk[1:], later)], -1))

    results = []
    for pair in range(2):
        rows = pl.pallas_call(
            unpack_kernel,
            out_shape=shape((SEQ, 2, 128, DH)),
            in_specs=[SMEM] + [ANY] * (RING + 1),
            out_specs=VMEM,
            scratch_shapes=[
                pltpu.VMEM((ROWS, 2, SPAN, DH), BF16),
                pltpu.SemaphoreType.DMA((RING,)),
            ],
            compiler_params=PARAMS,
            cost_estimate=cost(0, COST),
            name="unpack",
        )(send_table, *ordered(returned[pair]), kv_grads[1][0])
        results.append(exchange(rows, "seq"))

    d_kv = pl.pallas_call(
        join_kernel,
        out_shape=shape(kv_store.shape),
        grid=(BLK,),
        in_specs=[SMEM] + [pl.BlockSpec((1, 2, 128, DH), lambda b: (b, 0, 0, 0))] * 4,
        out_specs=pl.BlockSpec((1, 2, 2, 2, 128, DH), lambda b: (b, 0, 0, 0, 0, 0)),
        cost_estimate=cost(0, COST),
        name="join",
    )(place, kv_grads[0][0], kv_grads[1][0], kv_grads[0][1], kv_grads[1][1])
    attn_out = jnp.stack([results[0][:, 0], results[1][:, 0]], axis=1).reshape(query.shape)
    d_query = jnp.stack([results[0][:, 1], results[1][:, 1]], axis=1).reshape(query.shape)
    return (attn_out, d_query, d_kv)


def solution(mesh):
    in_specs = (
        P("grp", "store", None, "seq", None),
        P(("grp", "store"), None, None, "seq", None, None),
        P("grp", None, None),
        P("grp", None, None),
        P("grp", "store", None, "seq", None),
    )
    out_specs = (
        P("grp", "store", None, "seq", None),
        P("grp", "store", None, "seq", None),
        P(("grp", "store"), None, None, "seq", None, None),
    )
    return jax.shard_map(
        on_device, mesh=mesh, in_specs=in_specs, out_specs=out_specs, check_vma=False
    )
```

```python
import functools
import math

import jax
import jax.numpy as jnp
from jax import lax
from jax.experimental import pallas as pl
from jax.experimental.pallas import tpu as pltpu
from jax.sharding import PartitionSpec as P

RING = 8
CAP = 6
SLOTS = 2 * CAP
ROWS = RING * SLOTS
SPAN = 64
DH = 128
SEQ = 16
INST = 64
SPANS = INST // 2
BLK = 16
UNROLL = 8
UNROLL_STATS = 8
COST = 1 << 10
LIST = 104
SCALE = 1.0 / math.sqrt(DH)
F32 = jnp.float32
BF16 = jnp.bfloat16

SMEM = pl.BlockSpec(memory_space=pltpu.SMEM)
VMEM = pl.BlockSpec(memory_space=pltpu.VMEM)
ANY = pl.BlockSpec(memory_space=pltpu.HBM)

STAT_ROWS = ROWS
R_STAT, R_BLK, R_PAIR, R_COUNT, R_SIZE = 128, 256, 384, 512, 640


def cost(flops, nbytes):
    return pl.CostEstimate(flops=flops, bytes_accessed=nbytes, transcendentals=0)


def recv_table_kernel(place, names, table, count, where):
    def rank(source, carry):
        for o in range(RING * 2):
            count[o] = 0

        def step(i, carry):
            own = names[source, i]
            slot = (own & 1) * CAP + count[own]
            count[own] = count[own] + 1
            where[source * INST + i] = (own >> 1) * STAT_ROWS + source * SLOTS + slot
            return carry

        return lax.fori_loop(0, INST, step, carry, unroll=8)

    lax.fori_loop(0, RING, rank, 0)

    def group(source, total):
        def step(i, total):
            own = names[source, i]
            at = where[source * INST + i]
            local = at - (own >> 1) * STAT_ROWS
            table[total] = local + (((place[0] - source) & (RING - 1)) - source) * SLOTS
            table[R_STAT + total] = local
            table[R_BLK + total] = (own & 1) * BLK + names[source, INST + i]
            table[R_PAIR + total] = where[source * INST + (i ^ 1)]
            return total + ((own >> 1) == place[0]).astype(jnp.int32)

        return lax.fori_loop(0, INST, step, total, unroll=8)

    total = lax.fori_loop(0, RING, group, 0)

    def pad(n, carry):
        table[n] = ROWS
        table[R_STAT + n] = STAT_ROWS
        table[R_BLK + n] = 0
        table[R_PAIR + n] = 0
        return carry

    lax.fori_loop(total, LIST, pad, 0)
    table[R_COUNT] = total


def part_copies(stage, parts, sems, load):
    copies = []
    for n in range(RING):
        d = ORDER[n] if load else n
        rows = stage.at[pl.ds(d * SLOTS, SLOTS)]
        ends = (parts[n], rows) if load else (rows, parts[n])
        copies.append(pltpu.make_async_copy(*ends, sems.at[n]))
        copies[-1].start()
    return copies


def pack_kernel(place, names, rows, *refs):
    outs, (table, stage, count, sems) = refs[-RING - 4 : -4], refs[-4:]
    for o in range(RING * 2):
        count[o] = 0

    def step(i, carry):
        own = names[i]
        chip = ((own >> 1) - place[0]) & (RING - 1)
        row = chip * SLOTS + (own & 1) * CAP + count[own]
        count[own] = count[own] + 1
        table[i] = row
        span = i >> 1
        start = pl.multiple_of((span & 1) * SPAN, SPAN)
        for kind in range(2):
            stage[row, kind] = rows[span >> 1, kind, pl.ds(start, SPAN), :]
        return carry

    lax.fori_loop(0, INST, step, 0, unroll=4)
    for copy in part_copies(stage, outs, sems, False):
        copy.wait()


def gate_kernel(*refs):
    pass


def load_store(pair, core, own, other, store, sems):
    mine = pltpu.make_async_copy(
        own.at[:, :, core, pair], store.at[pl.ds(core * BLK, BLK)], sems.at[RING]
    )
    theirs = pltpu.make_async_copy(
        other.at[:, :, pair], store.at[pl.ds((1 - core) * BLK, BLK)], sems.at[RING + 1]
    )
    mine.start()
    theirs.start()
    return [mine, theirs]


def dot(a, b, dims):
    return lax.dot_general(a, b, (dims, ((), ())), preferred_element_type=F32)


NT = ((1,), (1,))
NN = ((1,), (0,))
TN = ((0,), (0,))


def load_all(pair, place, parts, own, other, stage, store, sems):
    copies = load_store(pair, place[1], own, other, store, sems)
    copies += part_copies(stage, parts, sems, True)
    stage[ROWS] = jnp.zeros(stage.shape[1:], BF16)
    return copies


def stat_kernel(pair, place, table, *refs):
    parts, own, other = refs[:RING], refs[RING], refs[RING + 1]
    out, stage, store, stats, sems = refs[-5:]
    copies = load_all(pair, place, parts, own, other, stage, store, sems)
    stats[...] = jnp.zeros(stats.shape, F32)
    for copy in copies:
        copy.wait()

    def step(it, carry):
        for u in range(UNROLL_STATS):
            n = it * UNROLL_STATS + u
            row, srow, block = table[n], table[R_STAT + n], table[R_BLK + n]
            score = dot(store[block, 0], stage[row, 0], NT) * SCALE
            gprob = dot(store[block, 1], stage[row, 1], NT)
            top = jnp.max(score, axis=0, keepdims=True)
            weight = jnp.exp(score - top)
            total = jnp.sum(weight, axis=0, keepdims=True)
            delta = jnp.sum(weight * gprob, axis=0, keepdims=True) / total
            stats[pl.ds(srow, 1), :] = jnp.concatenate([top + jnp.log(total), delta], axis=1)
        return carry

    lax.fori_loop(0, (table[R_COUNT] + UNROLL_STATS - 1) // UNROLL_STATS, step, 0)
    for chip in range(RING):
        out[pl.ds(chip * STAT_ROWS, STAT_ROWS), :] = stats[:STAT_ROWS]


def grad_kernel(pair, place, table, given, *refs):
    parts, own, other = refs[:RING], refs[RING], refs[RING + 1]
    outs = refs[-RING - 10 : -10]
    keep, send, stage, store, result, mine, theirs, stats, total, sems = refs[-10:]
    copies = load_all(pair, place, parts, own, other, stage, store, sems)
    base = place[0] * STAT_ROWS

    def take(n, carry):
        srow = jnp.minimum(table[R_STAT + n], STAT_ROWS - 1)
        mine[pl.ds(n, 1), :] = given[pl.ds(base + srow, 1), :]
        theirs[pl.ds(n, 1), :] = given[pl.ds(table[R_PAIR + n], 1), :]
        return carry

    lax.fori_loop(0, LIST, take, 0, unroll=8)
    log1, log2 = mine[:, :SPAN], theirs[:, :SPAN]
    top = jnp.maximum(log1, log2)
    both = top + jnp.log(jnp.exp(log1 - top) + jnp.exp(log2 - top))
    delta = jnp.exp(log1 - both) * mine[:, SPAN:] + jnp.exp(log2 - both) * theirs[:, SPAN:]
    merged = jnp.concatenate([both, delta], axis=1)
    used = lax.broadcasted_iota(jnp.int32, (LIST, DH), 0) < table[R_COUNT]
    stats[...] = jnp.where(used, merged, 0.0)

    def clear(b, carry):
        total[b] = jnp.zeros(total.shape[1:], F32)
        return carry

    lax.fori_loop(0, 2 * BLK, clear, 0)
    for copy in copies:
        copy.wait()

    def step(it, carry):
        adds = []
        for u in range(UNROLL):
            n = it * UNROLL + u
            row, block = table[n], table[R_BLK + n]
            query, grad = stage[row, 0], stage[row, 1]
            key, value = store[block, 0], store[block, 1]
            stat = stats[pl.ds(n, 1), :]
            score = dot(key, query, NT) * SCALE
            prob = jnp.exp(score - stat[:, :SPAN])
            dscore = (prob * (dot(value, grad, NT) - stat[:, SPAN:])).astype(BF16)
            prob = prob.astype(BF16)
            result[row, 0] = dot(prob, value, TN).astype(BF16)
            result[row, 1] = (dot(dscore, key, TN) * SCALE).astype(BF16)
            total[block, 0] += dot(dscore, query, NN)
            total[block, 1] += dot(prob, grad, NN)
        return carry

    lax.fori_loop(0, (table[R_COUNT] + UNROLL - 1) // UNROLL, step, 0)
    copies = part_copies(result, outs, sems, False)

    def finish(b, carry):
        for half, core in ((keep, place[1]), (send, 1 - place[1])):
            half[b, 0] = (total[core * BLK + b, 0] * SCALE).astype(BF16)
            half[b, 1] = total[core * BLK + b, 1].astype(BF16)
        return carry

    lax.fori_loop(0, BLK, finish, 0)
    for copy in copies:
        copy.wait()


def unpack_kernel(table, *refs):
    parts, (out, stage, sems) = refs[:RING], refs[-3:]
    for copy in part_copies(stage, parts, sems, True):
        copy.wait()
    def step(c, carry):
        one, two = table[2 * c], table[2 * c + 1]
        start = pl.multiple_of((c & 1) * SPAN, SPAN)
        for kind in range(2):
            summed = stage[one, kind].astype(F32) + stage[two, kind].astype(F32)
            out[c >> 1, kind, pl.ds(start, SPAN), :] = summed.astype(BF16)
        return carry

    lax.fori_loop(0, SPANS, step, 0, unroll=2)


def join_kernel(place, keep0, keep1, got0, got1, out):
    core = place[1]
    for ref, half, pair in (
        (keep0, core, 0),
        (keep1, core, 1),
        (got0, 1 - core, 0),
        (got1, 1 - core, 1),
    ):
        for kind in range(2):
            out[0, kind, half, pair] = ref[0, kind]


def shape(dims, dtype=BF16):
    return jax.ShapeDtypeStruct(dims, dtype)


PARAMS = pltpu.CompilerParams(vmem_limit_bytes=60 * 1024 * 1024)
PART = (SLOTS, 2, SPAN, DH)
STAGE = pltpu.VMEM((ROWS + 1, 2, SPAN, DH), BF16)
STORE = pltpu.VMEM((2 * BLK, 2, 128, DH), BF16)
SEMS = pltpu.SemaphoreType.DMA((RING + 2,))


EARLY = (4, 3, 5, 2, 6)
LIGHT, HEAVY = (2, 6, 1, 7), (4, 3, 5)
ORDER = (0, 4, 3, 5, 2, 6, 1, 7)


def exchange(rows, axis):
    return lax.all_to_all(rows, axis, split_axis=0, concat_axis=0, tiled=True)


def ring_send(parts, sign):
    got = list(parts)
    for d in sorted(range(1, RING), key=ORDER.index):
        pairs = [(i, (i + sign * d) % RING) for i in range(RING)]
        got[d] = lax.ppermute(parts[d], "grp", pairs)
    return got


def ordered(parts):
    return [parts[d] for d in ORDER]


def gate(parts, after):
    return pl.pallas_call(
        gate_kernel,
        out_shape=[shape(part.shape, part.dtype) for part in parts],
        in_specs=[ANY] * (len(parts) + len(after)),
        out_specs=[ANY] * len(parts),
        input_output_aliases={n + len(after): n for n in range(len(parts))},
        cost_estimate=cost(0, COST),
        name="gate",
    )(*after, *parts)


def on_device(query, kv_store, nbr_owner, nbr_block, d_out):
    core = lax.axis_index("store")
    place = jnp.stack([lax.axis_index("grp"), core]).astype(jnp.int32)
    names = jnp.concatenate([nbr_owner.reshape(INST), nbr_block.reshape(INST)])
    swap = [(0, 1), (1, 0)]
    query_rows = query.reshape(SEQ, 2, 128, DH)
    grad_rows = d_out.reshape(SEQ, 2, 128, DH)
    first = jnp.stack([query_rows[:, 0], grad_rows[:, 0]], axis=1)
    first, half = lax.optimization_barrier((first, 1 - core))
    kv_other = lax.ppermute(
        lax.dynamic_index_in_dim(kv_store, half, 2, keepdims=False), "store", swap
    )

    arrived = []
    all_names = lax.all_gather(names.reshape(1, 2 * INST), "grp", tiled=True)
    after = [kv_other, all_names]
    for pair in range(2):
        rows = first if pair == 0 else jnp.stack([query_rows[:, 1], grad_rows[:, 1]], axis=1)
        rows = exchange(rows, "seq")
        outs = pl.pallas_call(
            pack_kernel,
            out_shape=[shape(PART)] * RING
            + [shape((INST,), jnp.int32)],
            in_specs=[SMEM, SMEM, VMEM] + [ANY] * len(after),
            out_specs=[ANY] * RING + [SMEM],
            scratch_shapes=[
                pltpu.VMEM((ROWS, 2, SPAN, DH), BF16),
                pltpu.SMEM((2 * RING,), jnp.int32),
                pltpu.SemaphoreType.DMA((RING,)),
            ],
            compiler_params=PARAMS,
            cost_estimate=cost(0, COST),
            name="pack",
        )(place, names, rows, *after)
        send_table = outs[RING]
        if pair == 0:
            recv_table = pl.pallas_call(
                recv_table_kernel,
                out_shape=shape((R_SIZE,), jnp.int32),
                in_specs=[SMEM, SMEM],
                out_specs=SMEM,
                scratch_shapes=[
                    pltpu.SMEM((2 * RING,), jnp.int32),
                    pltpu.SMEM((RING * INST,), jnp.int32),
                ],
                cost_estimate=cost(0, COST),
                name="recv_table",
            )(place, all_names)
            arrived.append(ring_send(outs[:RING], 1))
            after = [recv_table] + [arrived[0][d] for d in EARLY]
    bulk = outs[:RING]

    after = [send_table]
    kv_grads = []
    returned = []
    for pair in range(2):
        stats = pl.pallas_call(
            functools.partial(stat_kernel, pair),
            out_shape=shape((RING * STAT_ROWS, DH), F32),
            in_specs=[SMEM, SMEM] + [ANY] * (RING + 2 + len(after)),
            out_specs=VMEM,
            scratch_shapes=[STAGE, STORE, pltpu.VMEM((STAT_ROWS + 8, DH), F32), SEMS],
            compiler_params=PARAMS,
            cost_estimate=cost(COST, COST),
            name="stats",
        )(place, recv_table, *ordered(arrived[pair]), kv_store, kv_other, *after)
        given = exchange(stats, "grp")
        bulk = list(bulk)
        for some, ready in ((LIGHT, stats), (HEAVY, given)):
            for d, part in zip(some, gate([bulk[d] for d in some], [ready])):
                bulk[d] = part
        moved = ring_send(bulk, 1 - 2 * pair)
        if pair == 0:
            arrived.append(moved)
        else:
            returned.append(moved)
        outs = pl.pallas_call(
            functools.partial(grad_kernel, pair),
            out_shape=[shape(PART)] * RING + [shape((BLK, 2, 128, DH))] * 2,
            in_specs=[SMEM, SMEM, VMEM] + [ANY] * (RING + 2 + len(LIGHT)),
            out_specs=[ANY] * RING + [VMEM] * 2,
            scratch_shapes=[STAGE, STORE, STAGE]
            + [pltpu.VMEM((LIST, DH), F32)] * 3
            + [pltpu.VMEM((2 * BLK, 2, 128, DH), F32), SEMS],
            compiler_params=PARAMS,
            cost_estimate=cost(COST, COST),
            name="grads",
        )(
            place,
            recv_table,
            given,
            *ordered(arrived[pair]),
            kv_store,
            kv_other,
            *(moved[d] for d in LIGHT),
        )
        bulk = outs[:RING]
        after = [outs[RING]]
        kv_grads.append((outs[RING], lax.ppermute(outs[RING + 1], "store", swap)))
    later = [returned[0][d] for d in LIGHT + HEAVY[:1]]
    returned.append(ring_send([bulk[0], *gate(bulk[1:], later)], -1))

    results = []
    for pair in range(2):
        rows = pl.pallas_call(
            unpack_kernel,
            out_shape=shape((SEQ, 2, 128, DH)),
            in_specs=[SMEM] + [ANY] * (RING + 1),
            out_specs=VMEM,
            scratch_shapes=[
                pltpu.VMEM((ROWS, 2, SPAN, DH), BF16),
                pltpu.SemaphoreType.DMA((RING,)),
            ],
            compiler_params=PARAMS,
            cost_estimate=cost(0, COST),
            name="unpack",
        )(send_table, *ordered(returned[pair]), kv_grads[1][0])
        results.append(exchange(rows, "seq"))

    d_kv = pl.pallas_call(
        join_kernel,
        out_shape=shape(kv_store.shape),
        grid=(BLK,),
        in_specs=[SMEM] + [pl.BlockSpec((1, 2, 128, DH), lambda b: (b, 0, 0, 0))] * 4,
        out_specs=pl.BlockSpec((1, 2, 2, 2, 128, DH), lambda b: (b, 0, 0, 0, 0, 0)),
        cost_estimate=cost(0, COST),
        name="join",
    )(place, kv_grads[0][0], kv_grads[1][0], kv_grads[0][1], kv_grads[1][1])
    attn_out = jnp.stack([results[0][:, 0], results[1][:, 0]], axis=1).reshape(query.shape)
    d_query = jnp.stack([results[0][:, 1], results[1][:, 1]], axis=1).reshape(query.shape)
    return (attn_out, d_query, d_kv)


def solution(mesh):
    in_specs = (
        P("grp", "store", None, "seq", None),
        P(("grp", "store"), None, None, "seq", None, None),
        P("grp", None, None),
        P("grp", None, None),
        P("grp", "store", None, "seq", None),
    )
    out_specs = (
        P("grp", "store", None, "seq", None),
        P("grp", "store", None, "seq", None),
        P(("grp", "store"), None, None, "seq", None, None),
    )
    return jax.shard_map(
        on_device, mesh=mesh, in_specs=in_specs, out_specs=out_specs, check_vma=False
    )
```
